256 devices in a mesh: sky: 32 (over z, x), exp: 8 (over y, core).
Axes of the slice: x: 4, y: 4, z: 8, core: 2. Of those that a mesh axis runs over, the one named last changes fastest.
Arguments:
- image: float32 [64, 1024, 2048], P('exp', 'sky'), may hold values from -6 to 6
- variance: float32 [64, 1024, 2048], P('exp', 'sky'), may hold values from 0.25 to 4
- coef_index: int32 [64], P('exp'), may hold values from 0 to 15
- coef_table: float32 [16, 5], replicated, may hold values from -3 to 3
- row_taps: float32 [5, 41], replicated, may hold values from -1 to 1
- col_taps: float32 [5, 41], replicated, may hold values from -1 to 1
- destination: int32 [8, 32, 64, 1], P('exp', 'sky'), may hold values from 0 to 31; in each aligned block of 64 rows (0 to 63, 64 to 127, ..., all dimensions but the last counted through in order) at most 4 rows name the same one
- offset: int32 [8, 32, 64], P('exp', 'sky'), may hold values from 0 to 120
Outputs:
- coadd: float32 [4096, 1024], P(('sky', 'exp'))
- weight_map: float32 [4096, 1024], P(('sky', 'exp'))
The draws below stay inside these ranges and needn't reach their ends.
Inputs may be any that keep to these rules, and one draw needn't show every extreme that they name: `destination`: among the strips of one device no patch is named more than 4 times, and some device names some patch exactly 4 times.
All inputs are finite; a program needn't handle non-finite values.
Results may differ from the reference program's by a relative error of at most 0.000082.
Values sent between devices are 32-bit elements; how exact they have to be, the bound alone decides.
A program may use at most 128 MiB of HBM per device.

```python
import math
import jax
import jax.numpy as jnp
import numpy as np
from jax import lax

NBASIS = 5
TAPS = 41
TC = 2048
SC = 1024
EXP_DEV = 8
TR_DEV = 32
SR = 8
PR = 128
NCOEF = 16
NEXP = 64
TR = 1024
STRIP_DEV = 64
MOST = 4
N_SKY = 32
N_EXP = 8


def place_ends(array, own_key, smallest, high):
    index_at = [jax.random.randint(jax.random.fold_in(own_key, axis), (), 0, length) for axis, length in enumerate(array.shape)]
    main_axis = array.shape.index(max(array.shape))
    beside = index_at[:main_axis] + [(index_at[main_axis] + 1) % array.shape[main_axis]] + index_at[main_axis + 1:]
    return array.at[tuple(index_at)].set(smallest).at[tuple(beside)].set(high)


def shard_levels(rng, dims, pieces, low, largest):
    loudness, own = 1.0, jax.random.fold_in(rng, 6)
    for position, parts in pieces:
        heights = jnp.exp(jax.random.uniform(jax.random.fold_in(own, position), (parts,), jnp.float32, low / len(pieces), largest / len(pieces)))
        loudness = loudness * jnp.repeat(heights, dims[position] // parts).reshape([-1 if axis == position else 1 for axis in range(len(dims))])
    return loudness


def assign_block(stream_key, own, number, rows, amount, top, bound, slope):
    sequence = jax.random.permutation(stream_key, amount)
    crowded, common = portions_of(amount, rows * top, bound, slope, True), portions_of(amount, rows * top, bound, slope, False)
    places = jnp.arange(amount)

    def named(lengths, turn):
        used = int((lengths > 0).sum())
        fixed = max(1, used // 4)
        shifted = fixed + (places - fixed + turn * (used - fixed)) % max(1, amount - fixed)
        return jnp.zeros((amount,), jnp.int32).at[sequence[jnp.where(places < fixed, places, shifted)]].set(jnp.asarray(lengths, jnp.int32))

    lengths = jnp.where(number % 4 == 0, named(crowded, number // 4), named(common, number - number // 4 - 1))
    mixed = jax.random.permutation(jax.random.fold_in(own, 3), amount)
    giver, receiver = mixed[0:amount // 2 * 2:2], mixed[1:amount // 2 * 2:2]
    margin = jnp.minimum(lengths[giver] - 1, bound - lengths[receiver]) // 2
    margin = jnp.where((giver == sequence[0]) | (receiver == sequence[0]) | (lengths[receiver] == 0), 0, jnp.maximum(margin, 0))
    shifted = jax.random.randint(jax.random.fold_in(own, 4), (amount // 2,), 0, 1 << 20) % (margin + 1)
    lengths = lengths.at[giver].add(-shifted).at[receiver].add(shifted)
    labels = jnp.searchsorted(jnp.cumsum(lengths), jnp.arange(rows * top), side="right").astype(jnp.int32)
    table = labels.reshape(top, rows).T
    table = table[jax.random.permutation(jax.random.fold_in(own, 1), rows)]
    turn = jax.random.randint(jax.random.fold_in(own, 2), (rows, 1), 0, top)
    return jnp.take_along_axis(table, (jnp.arange(top)[None, :] + turn) % top, axis=1)


def portions_of(count, total, limit, skew, full):
    loads = [(1 << 20) // math.isqrt(standing ** skew) + 1 for standing in range(1, count + 1)]
    largest = limit if full else min(limit, max(-(-total // count), total * loads[0] // sum(loads)))
    least = 1 if total - largest >= count - 1 else 0
    holding, rest = [largest] + [least] * (count - 1), total - largest - least * (count - 1)
    while rest > 0:
        free = [i for i in range(1, count) if holding[i] < largest] or [i for i in range(1, count) if holding[i] < limit]
        mass, remaining = sum([loads[i] for i in free]), rest
        for i in free:
            extra = min(limit - holding[i], max(1, remaining * loads[i] // mass), rest)
            holding[i] = holding[i] + extra
            rest = rest - extra
    return np.array(holding)


def noise(stream_key, dims, scale, limit, cuts=(), held_as=jnp.bfloat16):
    gain = shard_levels(stream_key, dims, cuts, -0.22, 0.18) if cuts else 1.0
    values = jax.random.normal(stream_key, dims, jnp.float32) * scale * gain
    return jnp.minimum(jnp.maximum(values, -limit), limit).astype(held_as)


def setup_inputs(seed: int = 0) -> dict:
    seeds = jax.random.split(jax.random.key(seed), 9)
    image = noise(seeds[0], (NEXP, TR, TC), 1.0, 6.0, ((0, 8), (1, 32)), jnp.float32)
    variance = jnp.clip(jnp.exp(math.log(4.0) - 2.7725887 * jax.random.uniform(seeds[1], (NEXP, TR, TC), jnp.float32) ** shard_levels(seeds[1], (NEXP, TR, TC), ((0, 8), (1, 32)), -0.2, 0.2)), 0.25, 4.0)
    coef_index = place_ends(jax.random.randint(seeds[2], (NEXP,), 0, NCOEF), jax.random.fold_in(seeds[2], 1), 0, NCOEF - 1).astype(jnp.int32)
    coef_table = noise(seeds[3], (NCOEF, NBASIS), 0.6, 3.0, (), jnp.float32)
    row_taps = noise(seeds[4], (NBASIS, TAPS), TAPS ** -0.5, 1.0, (), jnp.float32)
    col_taps = noise(seeds[5], (NBASIS, TAPS), TAPS ** -0.5, 1.0, (), jnp.float32)
    destination_keys = jax.random.split(jax.random.fold_in(seeds[6], 1), N_EXP * N_SKY * STRIP_DEV // STRIP_DEV)
    destination_turns = jax.random.permutation(jax.random.fold_in(seeds[6], 3), N_EXP * N_SKY * STRIP_DEV // STRIP_DEV)
    destination = jax.vmap(lambda own, number: assign_block(jax.random.fold_in(seeds[6], 2), own, number, STRIP_DEV, N_SKY, 1, MOST, 2))(destination_keys, destination_turns).reshape((N_EXP, N_SKY, STRIP_DEV, 1))
    offset = place_ends(jax.random.randint(seeds[7], (N_EXP, N_SKY, STRIP_DEV), 0, PR - SR + 1), jax.random.fold_in(seeds[7], 1), 0, PR - SR).astype(jnp.int32)
    return {"image": image, "variance": variance, "coef_index": coef_index, "coef_table": coef_table, "row_taps": row_taps, "col_taps": col_taps, "destination": destination, "offset": offset}


def convolve_tile(tile, factors, row_taps, col_taps):
    half = (TAPS - 1) // 2
    source = tile[None, None]
    horizontal = col_taps[:, None, None, :]
    first = lax.conv_general_dilated(source, horizontal, (1, 1), ((0, 0), (half, half)), precision=lax.Precision.HIGHEST)
    vertical = row_taps[:, None, :, None]
    second = lax.conv_general_dilated(first, vertical, (1, 1), ((half, half), (0, 0)), feature_group_count=NBASIS, precision=lax.Precision.HIGHEST)
    return jnp.einsum("b,byx->yx", factors, second[0], precision=lax.Precision.HIGHEST)


def to_strips(field):
    shaped = field.reshape(N_EXP, EXP_DEV, N_SKY, TR_DEV // SR, SR, 2, SC)
    return shaped.transpose(0, 2, 1, 3, 5, 4, 6).reshape(-1, SR, SC)


def reference(image, variance, coef_index, coef_table, row_taps, col_taps, destination, offset):
    coefficients = coef_table[coef_index]
    matched = lax.map(lambda pair: convolve_tile(pair[0], pair[1], row_taps, col_taps), (image, coefficients))
    weight = 1.0 / variance
    weighted = weight * matched
    first_row = destination.reshape(-1).astype(jnp.int32) * PR + offset.reshape(-1).astype(jnp.int32)
    targets = (first_row[:, None] + jnp.arange(SR, dtype=jnp.int32)[None, :]).reshape(-1)
    weighted_sum = jax.ops.segment_sum(to_strips(weighted).reshape(-1, SC), targets, N_SKY * PR)
    weight_map = jax.ops.segment_sum(to_strips(weight).reshape(-1, SC), targets, N_SKY * PR)
    coadd = weighted_sum / (1.0 + weight_map)
    return coadd, weight_map
```

```python
import jax
import jax.numpy as jnp
from jax import lax
from jax.experimental import pallas as pl
from jax.experimental.pallas import tpu as pltpu
from jax.sharding import PartitionSpec as P

MESH = pl.DeviceIdType.MESH
F32, BF16, I32 = jnp.float32, jnp.bfloat16, jnp.int32

NB, TAPS, RIM = 5, 41, 20
N_SKY, N_EXP, NX, NZ = 32, 8, 4, 8
EXPS, ROWS, COLS, HALF = 8, 32, 2048, 1024
BLOCKS = EXPS * ROWS // 8
LANES = 128
PR, PATCH_ROWS = 128, 4096
PER = 4
CHUNKS = EXPS // PER
STEP = 256
NSTEP = COLS // STEP


def iota(shape, dim):
    return lax.broadcasted_iota(I32, shape, dim)


def greet(devices):
    barrier = pltpu.get_barrier_semaphore()
    for device in devices:
        pl.semaphore_signal(barrier, inc=1, device_id=device, device_id_type=MESH)
    pl.semaphore_wait(barrier, len(devices))


def split(value):
    high = value.astype(BF16)
    return high, (value - high.astype(F32)).astype(BF16)


def match_kernel(
    image, variance, dest, offs, coef_index, coef_table, row_taps, col_taps,
    out_w, out_v, out_m,
    h_send, h_recv, w_buf, v_buf, m_buf, z_hi, z_lo, h_hi, h_lo, v_base,
    halo_s, halo_r, w_s, w_r, v_s, v_r, m_s, m_r, own_s,
):
    sky, exp = lax.axis_index("sky"), lax.axis_index("exp")
    after, before = lax.rem(sky + 1, N_SKY), lax.rem(sky + N_SKY - 1, N_SKY)
    peers = [lax.rem(exp + d, N_EXP) for d in range(N_EXP)]

    m_buf[...] = jnp.zeros((8, LANES), I32)
    m_buf[0:1, 0:64] = dest[...] * PR + offs[...]
    low_half = iota((8, HALF), 0) < 4

    def pack(e, _):
        h_send[0, e, 0] = image[e, 16:24, 0:HALF]
        h_send[0, e, 1] = image[e, 24:32, 0:HALF]
        h_send[0, e, 2] = image[e, 16:24, HALF:COLS]
        h_send[0, e, 3] = image[e, 24:32, HALF:COLS]
        h_send[0, e, 4] = jnp.where(
            low_half, pltpu.roll(image[e, 8:16, HALF:COLS], 4, 0), image[e, 8:16, 0:HALF]
        )
        h_send[1, e, 0] = image[e, 0:8, 0:HALF]
        h_send[1, e, 1] = image[e, 8:16, 0:HALF]
        h_send[1, e, 2] = image[e, 0:8, HALF:COLS]
        h_send[1, e, 3] = image[e, 8:16, HALF:COLS]
        h_send[1, e, 4] = jnp.where(
            low_half, image[e, 16:24, 0:HALF], pltpu.roll(image[e, 16:24, HALF:COLS], 4, 0)
        )
        return 0

    lax.fori_loop(0, EXPS, pack, 0)

    greet([(after, exp), (before, exp)] + [(sky, q) for q in peers[1:]])

    def halo(direction, e):
        return pltpu.make_async_remote_copy(
            src_ref=h_send.at[direction, e],
            dst_ref=h_recv.at[direction, e],
            send_sem=halo_s.at[direction, e],
            recv_sem=halo_r.at[direction, e],
            device_id=(after if direction == 0 else before, exp),
            device_id_type=MESH,
        )

    def start_halo(e, _):
        halo(0, e).start()
        halo(1, e).start()
        return 0

    lax.fori_loop(0, EXPS, start_halo, 0)

    def meta(d):
        return pltpu.make_async_remote_copy(
            src_ref=m_buf, dst_ref=out_m.at[exp], send_sem=m_s.at[d], recv_sem=m_r.at[d],
            device_id=(sky, peers[d]), device_id_type=MESH,
        )

    for d in range(1, N_EXP):
        meta(d).start()

    def weights(eb, _):
        e, rb = eb // 4, lax.rem(eb, 4)
        rows = pl.ds(pl.multiple_of(rb * 8, 8), 8)
        for part in range(2):
            for q in range(N_EXP):
                lane = part * HALF + q * LANES
                w_buf[q, eb, part] = 1.0 / variance[e, rows, lane:lane + LANES]
        return 0

    lax.fori_loop(0, BLOCKS, weights, 0)

    def send_w(d):
        return pltpu.make_async_remote_copy(
            src_ref=w_buf.at[peers[d]], dst_ref=out_w.at[exp], send_sem=w_s.at[d], recv_sem=w_r.at[d],
            device_id=(sky, peers[d]), device_id_type=MESH,
        )

    for d in range(1, N_EXP):
        send_w(d).start()

    own_w = pltpu.make_async_copy(w_buf.at[exp], out_w.at[exp], own_s.at[0])
    own_m = pltpu.make_async_copy(m_buf, out_m.at[exp], own_s.at[1])
    own_w.start()
    own_m.start()

    k3 = iota((ROWS, STEP), 1)
    k = lax.rem(k3, 80)
    source = jnp.where(
        k < 32, k, jnp.where(k < 48, k - 48, jnp.where(k < 68, k - 16, jnp.where(k < 72, k - 88, 1000)))
    )
    source = jnp.where(k3 < 240, source, 1000)
    source = jnp.where((source < 0) & (sky == 0), 1000, source)
    source = jnp.where((source >= ROWS) & (sky == N_SKY - 1), 1000, source)
    row_lag = source - iota((ROWS, STEP), 0) + RIM

    def row_band(b, _):
        def tap(t, band):
            return jnp.where(row_lag == t, row_taps[b, t], band)

        v_base[b] = lax.fori_loop(0, TAPS, tap, jnp.zeros((ROWS, STEP), F32))
        return 0

    lax.fori_loop(0, NB, row_band, 0)

    h_hi[...] = jnp.zeros(h_hi.shape, BF16)
    h_lo[...] = jnp.zeros(h_lo.shape, BF16)
    col_diff = iota((LANES, LANES), 0) - iota((LANES, LANES), 1) + RIM

    def col_band(b, _):
        for shift in (-1, 0, 1):
            lag = col_diff + LANES * shift

            def tap(t, band):
                return jnp.where(lag == t, col_taps[b, t], band)

            high, low = split(lax.fori_loop(0, TAPS, tap, jnp.zeros((LANES, LANES), F32)))
            for u in range(2):
                rows = slice((u + 1 + shift) * LANES, (u + 2 + shift) * LANES)
                h_hi[b, rows, u * LANES:(u + 1) * LANES] = high
                h_lo[b, rows, u * LANES:(u + 1) * LANES] = low
        return 0

    lax.fori_loop(0, NB, col_band, 0)

    for z in (z_hi, z_lo):
        z[:, :, 0:LANES] = jnp.zeros((NB, PER * ROWS, LANES), BF16)
        z[:, :, LANES + COLS:] = jnp.zeros((NB, PER * ROWS, LANES), BF16)

    third = lax.broadcasted_iota(I32, (NB * ROWS, STEP), 1) >= 160
    low_rows = iota((8, STEP), 0) < 4

    def send_v(c, d):
        span = pl.ds(c * (4 * PER), 4 * PER)
        return pltpu.make_async_remote_copy(
            src_ref=v_buf.at[peers[d], span], dst_ref=out_v.at[exp, span],
            send_sem=v_s.at[c, d], recv_sem=v_r.at[c, d],
            device_id=(sky, peers[d]), device_id_type=MESH,
        )

    def chunk(c, _):
        def vertical(el, _):
            e = c * PER + el
            halo(0, e).wait_recv()
            halo(1, e).wait_recv()
            table_row = coef_index[e]
            bands = [coef_table[table_row, b] * v_base[b] for b in range(NB)]
            high, low = split(jnp.concatenate(bands, 0))
            left = jnp.where(third, low.astype(F32), high.astype(F32)).astype(BF16)
            out_rows = pl.ds(pl.multiple_of(el * ROWS, ROWS), ROWS)
            for j in range(NSTEP):
                part, at = divmod(j * STEP, HALF)
                cols = slice(at, at + STEP)
                up = h_recv[0, e, 2 * part:2 * part + 2, :, cols].reshape(16, STEP)
                down = h_recv[1, e, 2 * part:2 * part + 2, :, cols].reshape(16, STEP)
                up4, down4 = h_recv[0, e, 4, :, cols], h_recv[1, e, 4, :, cols]
                if part == 0:
                    rest = jnp.where(low_rows, down4, up4)
                else:
                    rest = pltpu.roll(jnp.where(low_rows, up4, down4), 4, 0)
                x = jnp.concatenate(
                    [image[e, :, j * STEP:(j + 1) * STEP], up, down, rest, jnp.zeros((8, STEP), F32)], 0
                )
                x_hi, x_lo = split(x)
                right = jnp.concatenate([x_hi, x_lo, x_hi, jnp.zeros((16, STEP), BF16)], 0)
                z = jnp.dot(left, right, preferred_element_type=F32)
                high_z, low_z = split(z)
                at = LANES + j * STEP
                z_hi[:, out_rows, at:at + STEP] = high_z.reshape(NB, ROWS, STEP)
                z_lo[:, out_rows, at:at + STEP] = low_z.reshape(NB, ROWS, STEP)
            return 0

        lax.fori_loop(0, PER, vertical, 0)

        def horizontal(j, _):
            cols = pl.ds(pl.multiple_of(j * STEP, STEP), 2 * STEP)
            total = jnp.zeros((PER * ROWS, STEP), F32)
            for b in range(NB):
                zh, zl = z_hi[b, :, cols], z_lo[b, :, cols]
                total += jnp.dot(zh, h_hi[b], preferred_element_type=F32)
                total += jnp.dot(zl, h_hi[b], preferred_element_type=F32)
                total += jnp.dot(zh, h_lo[b], preferred_element_type=F32)
            part = j // 4
            span = pl.ds(c * (4 * PER), 4 * PER)
            for u in range(2):
                q = lax.rem(j, 4) * 2 + u
                piece = total[:, u * LANES:(u + 1) * LANES].reshape(4 * PER, 8, LANES)
                v_buf[q, span, part] = piece * w_buf[q, span, part]
            return 0

        lax.fori_loop(0, NSTEP, horizontal, 0)
        for d in range(1, N_EXP):
            send_v(c, d).start()
        return 0

    lax.fori_loop(0, CHUNKS, chunk, 0)

    own_v = pltpu.make_async_copy(v_buf.at[exp], out_v.at[exp], own_s.at[2])
    own_v.start()

    def end_halo(e, _):
        halo(0, e).wait_send()
        halo(1, e).wait_send()
        return 0

    lax.fori_loop(0, EXPS, end_halo, 0)
    for d in range(1, N_EXP):
        meta(d).wait()
        send_w(d).wait()
    own_w.wait()
    own_m.wait()
    own_v.wait()

    def end_v(c, _):
        for d in range(1, N_EXP):
            send_v(c, d).wait()
        return 0

    lax.fori_loop(0, CHUNKS, end_v, 0)


def match(image, variance, dest, offs, coef_index, coef_table, row_taps, col_taps):
    slabs = jax.ShapeDtypeStruct((N_EXP, BLOCKS, 2, 8, LANES), F32)
    vmem, smem, anywhere = (pl.BlockSpec(memory_space=s) for s in (pltpu.VMEM, pltpu.SMEM, pl.ANY))
    dma = pltpu.SemaphoreType.DMA
    return pl.pallas_call(
        match_kernel,
        out_shape=(slabs, slabs, jax.ShapeDtypeStruct((N_EXP, 8, LANES), I32)),
        in_specs=[vmem] * 4 + [smem] * 4,
        out_specs=(anywhere,) * 3,
        scratch_shapes=[
            pltpu.VMEM((2, EXPS, 5, 8, HALF), F32),
            pltpu.VMEM((2, EXPS, 5, 8, HALF), F32),
            pltpu.VMEM((N_EXP, BLOCKS, 2, 8, LANES), F32),
            pltpu.VMEM((N_EXP, BLOCKS, 2, 8, LANES), F32),
            pltpu.VMEM((8, LANES), I32),
            pltpu.VMEM((NB, PER * ROWS, COLS + 2 * LANES), BF16),
            pltpu.VMEM((NB, PER * ROWS, COLS + 2 * LANES), BF16),
            pltpu.VMEM((NB, 2 * STEP, STEP), BF16),
            pltpu.VMEM((NB, 2 * STEP, STEP), BF16),
            pltpu.VMEM((NB, ROWS, STEP), F32),
            dma((2, EXPS)), dma((2, EXPS)),
            dma((N_EXP,)), dma((N_EXP,)),
            dma((CHUNKS, N_EXP)), dma((CHUNKS, N_EXP)),
            dma((N_EXP,)), dma((N_EXP,)),
            dma((3,)),
        ],
        compiler_params=pltpu.CompilerParams(
            collective_id=0, has_side_effects=True, vmem_limit_bytes=50 * 1024 * 1024
        ),
    )(image, variance, dest, offs, coef_index, coef_table, row_taps, col_taps)


def place_kernel(rows, w, v, acc_w, acc_v):
    acc_w[...] = jnp.zeros((PATCH_ROWS, LANES), F32)
    acc_v[...] = jnp.zeros((PATCH_ROWS, LANES), F32)

    def group(source, _):
        def block(eb, _):
            for part in range(2):
                at = pl.ds(rows[source, 0, eb * 2 + part], 8)
                acc_w[at, :] += w[source, eb, part]
                acc_v[at, :] += v[source, eb, part]
            return 0

        return lax.fori_loop(0, BLOCKS, block, 0, unroll=4)

    lax.fori_loop(0, N_EXP, group, 0)


def place(rows, w, v):
    vmem, smem = (pl.BlockSpec(memory_space=s) for s in (pltpu.VMEM, pltpu.SMEM))
    dense = jax.ShapeDtypeStruct((PATCH_ROWS, LANES), F32)
    return pl.pallas_call(
        place_kernel,
        out_shape=(dense, dense),
        in_specs=[smem, vmem, vmem],
        out_specs=(vmem, vmem),
        compiler_params=pltpu.CompilerParams(vmem_limit_bytes=40 * 1024 * 1024),
    )(rows, w, v)


class Ring:
    def __init__(self, size, me, target, chunk, half, land, send, recv):
        self.size, self.me, self.target = size, me, target
        self.chunk, self.half, self.land = chunk, half, land
        self.send, self.recv = send, recv
        self.steps = size // 2

    def owner(self, way, distance):
        return lax.rem(self.me + (distance if way == 0 else self.size - distance), self.size)

    def copy(self, src, dst, way, number):
        return pltpu.make_async_remote_copy(
            src_ref=src, dst_ref=dst, send_sem=self.send.at[way, number], recv_sem=self.recv.at[way, number],
            device_id=self.target(self.owner(way, 1)), device_id_type=MESH,
        )

    def copies(self, way, step):
        own = self.chunk(self.owner(way, self.steps - step))
        here = self.land.at[way, step]
        if step == 0:
            return [self.copy(self.half(own, way), self.half(here, way), way, 0)], []
        came = self.land.at[way, step - 1]
        if step == 1:
            early = [self.copy(self.half(own, 1 - way), self.half(here, 1 - way), way, 1)]
            return early, [self.copy(self.half(came, way), self.half(here, way), way, 2)]
        return [], [self.copy(came, here, way, step + 1)]

    def begin(self):
        for step in (0, 1):
            for way in (0, 1):
                for copy in self.copies(way, step)[0]:
                    copy.start()

    def arrived(self, way, step):
        early, late = self.copies(way, step)
        for copy in early + late:
            copy.wait_recv()

    def advance(self, step):
        for way in (0, 1):
            self.arrived(way, step - 1)
            came = self.land.at[way, step - 1]
            own = self.chunk(self.owner(way, self.steps - step))
            if step == 1:
                came, own = self.half(came, way), self.half(own, way)
            came[...] = came[...] + own[...]
            for copy in self.copies(way, step)[1]:
                copy.start()

    def total(self):
        last = self.steps - 1
        for way in (0, 1):
            self.arrived(way, last)
        return self.chunk(self.me)[...] + self.land[0, last] + self.land[1, last]

    def drain(self):
        for step in range(self.steps):
            for way in (0, 1):
                early, late = self.copies(way, step)
                for copy in early + late:
                    copy.wait_send()


def gather_kernel(
    acc_w, acc_v, out_c, out_w,
    land1, land2, land3, land4, mid_v, mid_w, last, rows,
    s1, r1, s2, r2, s3, r3, s4, r4, row_s, row_r,
):
    sky, exp = lax.axis_index("sky"), lax.axis_index("exp")
    z, x = sky // NX, lax.rem(sky, NX)
    peers = [lax.rem(exp + d, N_EXP) for d in range(N_EXP)]

    def at_x(other):
        return (z * NX + other, exp)

    def at_z(other):
        return (other * NX + x, exp)

    greet(
        [at_x(lax.rem(x + 1, NX)), at_x(lax.rem(x + NX - 1, NX)),
         at_z(lax.rem(z + 1, NZ)), at_z(lax.rem(z + NZ - 1, NZ))]
        + [(sky, q) for q in peers[1:]]
    )

    def halves(size):
        def half(ref, which):
            return ref.at[which * size:(which + 1) * size]

        return half

    v_x = Ring(NX, x, at_x, lambda o: acc_v.at[:, o], halves(NZ // 2), land1, s1, r1)
    w_z = Ring(NZ, z, at_z, lambda o: acc_w.at[o], halves(NX // 2), land2, s2, r2)
    v_z = Ring(NZ, z, at_z, lambda o: mid_v.at[o], halves(PR // 2), land3, s3, r3)
    w_x = Ring(NX, x, at_x, lambda o: mid_w.at[o], halves(PR // 2), land4, s4, r4)

    w_z.begin()
    v_x.begin()
    w_z.advance(1)
    v_x.advance(1)
    w_z.advance(2)
    mid_v[...] = v_x.total()
    w_z.advance(3)
    v_z.begin()
    v_z.advance(1)
    mid_w[...] = w_z.total()
    w_x.begin()
    v_z.advance(2)
    w_x.advance(1)
    v_z.advance(3)
    weight = w_x.total()
    last[1] = weight
    last[0] = v_z.total() / (1.0 + weight)

    def rows_copy(d):
        return pltpu.make_async_remote_copy(
            src_ref=last.at[:, pl.ds(pl.multiple_of(peers[d] * 16, 16), 16)],
            dst_ref=rows.at[exp],
            send_sem=row_s.at[d], recv_sem=row_r.at[d],
            device_id=(sky, peers[d]), device_id_type=MESH,
        )

    for d in range(1, N_EXP):
        rows_copy(d).start()
    rows[exp] = last[:, pl.ds(pl.multiple_of(exp * 16, 16), 16)]
    for d in range(1, N_EXP):
        rows_copy(d).wait_recv()
    for q in range(N_EXP):
        out_c[:, q * LANES:(q + 1) * LANES] = rows[q, 0]
        out_w[:, q * LANES:(q + 1) * LANES] = rows[q, 1]
    for d in range(1, N_EXP):
        rows_copy(d).wait_send()
    for ring in (v_x, w_z, v_z, w_x):
        ring.drain()


def gather(acc_w, acc_v):
    vmem = pl.BlockSpec(memory_space=pltpu.VMEM)
    out = jax.ShapeDtypeStruct((PR // N_EXP, HALF), F32)
    dma = pltpu.SemaphoreType.DMA
    return pl.pallas_call(
        gather_kernel,
        out_shape=(out, out),
        in_specs=[vmem, vmem],
        out_specs=(vmem, vmem),
        scratch_shapes=[
            pltpu.VMEM((2, 2, NZ, PR, LANES), F32),
            pltpu.VMEM((2, 4, NX, PR, LANES), F32),
            pltpu.VMEM((2, 4, PR, LANES), F32),
            pltpu.VMEM((2, 2, PR, LANES), F32),
            pltpu.VMEM((NZ, PR, LANES), F32),
            pltpu.VMEM((NX, PR, LANES), F32),
            pltpu.VMEM((2, PR, LANES), F32),
            pltpu.VMEM((N_EXP, 2, PR // N_EXP, LANES), F32),
            dma((2, 3)), dma((2, 3)), dma((2, 5)), dma((2, 5)),
            dma((2, 5)), dma((2, 5)), dma((2, 3)), dma((2, 3)),
            dma((N_EXP,)), dma((N_EXP,)),
        ],
        compiler_params=pltpu.CompilerParams(
            collective_id=1, has_side_effects=True, vmem_limit_bytes=40 * 1024 * 1024
        ),
    )(acc_w.reshape(NZ, NX, PR, LANES), acc_v.reshape(NZ, NX, PR, LANES))


def per_device(image, variance, coef_index, coef_table, row_taps, col_taps, destination, offset):
    slab_w, slab_v, rows = match(
        image, variance, destination.reshape(1, -1), offset.reshape(1, -1),
        coef_index, coef_table, row_taps, col_taps,
    )
    acc_w, acc_v = place(rows, slab_w, slab_v)
    return gather(acc_w, acc_v)


def solution(mesh):
    placed = (
        P("exp", "sky", None),
        P("exp", "sky", None),
        P("exp"),
        P(),
        P(),
        P(),
        P("exp", "sky", None, None),
        P("exp", "sky", None),
    )
    return jax.shard_map(
        per_device,
        mesh=mesh,
        in_specs=placed,
        out_specs=(P(("sky", "exp"), None), P(("sky", "exp"), None)),
        check_vma=False,
    )
```

```python
import jax
import jax.numpy as jnp
from jax import lax
from jax.experimental import pallas as pl
from jax.experimental.pallas import tpu as pltpu
from jax.sharding import PartitionSpec as P

MESH = pl.DeviceIdType.MESH
F32, BF16, I32 = jnp.float32, jnp.bfloat16, jnp.int32

NB, TAPS, RIM = 5, 41, 20
N_SKY, N_EXP, NX, NZ = 32, 8, 4, 8
EXPS, ROWS, COLS, HALF = 8, 32, 2048, 1024
BLOCKS = EXPS * ROWS // 8
LANES = 128
PR, PATCH_ROWS = 128, 4096
PER = 4
CHUNKS = EXPS // PER
STEP = 256
NSTEP = COLS // STEP


def iota(shape, dim):
    return lax.broadcasted_iota(I32, shape, dim)


def greet(devices):
    barrier = pltpu.get_barrier_semaphore()
    for device in devices:
        pl.semaphore_signal(barrier, inc=1, device_id=device, device_id_type=MESH)
    pl.semaphore_wait(barrier, len(devices))


def split(value):
    high = value.astype(BF16)
    return high, (value - high.astype(F32)).astype(BF16)

SLOTS = 4
EMPTY = -4096


def strip_table(dest, offs):
    sub, lane = iota((64, LANES), 0), iota((64, LANES), 1)
    line = jnp.concatenate([dest, jnp.full((1, 64), -1, I32)], 1)
    shift = jnp.concatenate([offs, jnp.zeros((1, 64), I32)], 1)
    diagonal = sub == lane
    patch = jnp.sum(jnp.where(diagonal, line, 0), 1, keepdims=True)
    first = jnp.sum(jnp.where(diagonal, shift, 0), 1, keepdims=True)
    rank = jnp.sum(jnp.where((patch == line) & (lane < sub), 1, 0), 1, keepdims=True)
    here = patch * SLOTS + rank == lane
    strip = jnp.sum(jnp.where(here, sub, 0), 0, keepdims=True)
    start = jnp.sum(jnp.where(here, first - EMPTY, 0), 0, keepdims=True) + EMPTY
    row = iota((8, LANES), 0)
    return jnp.where(row == 0, strip, jnp.where(row == 1, start, 0))


class Ring:
    def __init__(self, size, me, target, chunk, half, land, send, recv):
        self.size, self.me, self.target = size, me, target
        self.chunk, self.half, self.land = chunk, half, land
        self.send, self.recv = send, recv
        self.steps = size // 2

    def owner(self, way, distance):
        return lax.rem(self.me + (distance if way == 0 else self.size - distance), self.size)

    def copy(self, src, dst, way, number):
        return pltpu.make_async_remote_copy(
            src_ref=src, dst_ref=dst, send_sem=self.send.at[way, number], recv_sem=self.recv.at[way, number],
            device_id=self.target(self.owner(way, 1)), device_id_type=MESH,
        )

    def copies(self, way, step):
        own = self.chunk(self.owner(way, self.steps - step))
        here = self.land.at[way, step]
        if step == 0:
            return [self.copy(self.half(own, way), self.half(here, way), way, 0)], []
        came = self.land.at[way, step - 1]
        if step == 1:
            early = [self.copy(self.half(own, 1 - way), self.half(here, 1 - way), way, 1)]
            return early, [self.copy(self.half(came, way), self.half(here, way), way, 2)]
        return [], [self.copy(came, here, way, step + 1)]

    def begin(self):
        for step in (0, 1):
            for way in (0, 1):
                for copy in self.copies(way, step)[0]:
                    copy.start()

    def arrived(self, way, step):
        early, late = self.copies(way, step)
        for copy in early + late:
            copy.wait_recv()

    def advance(self, step):
        for way in (0, 1):
            self.arrived(way, step - 1)
            came = self.land.at[way, step - 1]
            own = self.chunk(self.owner(way, self.steps - step))
            if step == 1:
                came, own = self.half(came, way), self.half(own, way)
            came[...] = came[...] + own[...]
            for copy in self.copies(way, step)[1]:
                copy.start()

    def total(self):
        last = self.steps - 1
        for way in (0, 1):
            self.arrived(way, last)
        return self.chunk(self.me)[...] + self.land[0, last] + self.land[1, last]

    def drain(self):
        for step in range(self.steps):
            for way in (0, 1):
                early, late = self.copies(way, step)
                for copy in early + late:
                    copy.wait_send()


def coadd_kernel(
    image_in, variance_in, dest, offs, coef_index, coef_table, row_taps, col_taps,
    out,
    image, variance, h_send, h_recv, w_buf, v_buf, w_got, v_got, m_buf, m_got, m_smem, slots,
    z_hi, z_lo, h_hi, h_lo, v_base, acc_w, acc_v,
    land_wz, land_wx, land_ax, land_az, land_bz, land_bx, mid_w, mid_a, mid_b, fin_w, fin_v, rows_w, rows_v,
    load_s, halo_s, halo_r, w_s, w_r, v_s, v_r, m_s, m_r, own_s,
    wz_s, wz_r, wx_s, wx_r, ax_s, ax_r, az_s, az_r, bz_s, bz_r, bx_s, bx_r, rw_s, rw_r, rv_s, rv_r,
):
    sky, exp = lax.axis_index("sky"), lax.axis_index("exp")
    z, x = sky // NX, lax.rem(sky, NX)
    after, before = lax.rem(sky + 1, N_SKY), lax.rem(sky + N_SKY - 1, N_SKY)
    peers = [lax.rem(exp + d, N_EXP) for d in range(N_EXP)]

    def at_x(other):
        return (z * NX + other, exp)

    def at_z(other):
        return (other * NX + x, exp)

    load_image = pltpu.make_async_copy(image_in, image, load_s.at[0])
    load_variance = pltpu.make_async_copy(variance_in, variance, load_s.at[1])
    load_image.start()
    load_variance.start()

    partners = [(after, exp), (before, exp)] + [(sky, q) for q in peers[1:]] + [
        at_x(lax.rem(x + 1, NX)), at_x(lax.rem(x + NX - 1, NX)),
        at_z(lax.rem(z + 1, NZ)), at_z(lax.rem(z + NZ - 1, NZ)),
    ]
    barrier = pltpu.get_barrier_semaphore()
    for device in partners:
        pl.semaphore_signal(barrier, inc=1, device_id=device, device_id_type=MESH)

    m_buf[...] = strip_table(dest[...], offs[...])
    load_image.wait()
    low_half = iota((8, HALF), 0) < 4

    def pack(e, _):
        h_send[0, e, 0] = image[e, 16:24, 0:HALF]
        h_send[0, e, 1] = image[e, 24:32, 0:HALF]
        h_send[0, e, 2] = image[e, 16:24, HALF:COLS]
        h_send[0, e, 3] = image[e, 24:32, HALF:COLS]
        h_send[0, e, 4] = jnp.where(
            low_half, pltpu.roll(image[e, 8:16, HALF:COLS], 4, 0), image[e, 8:16, 0:HALF]
        )
        h_send[1, e, 0] = image[e, 0:8, 0:HALF]
        h_send[1, e, 1] = image[e, 8:16, 0:HALF]
        h_send[1, e, 2] = image[e, 0:8, HALF:COLS]
        h_send[1, e, 3] = image[e, 8:16, HALF:COLS]
        h_send[1, e, 4] = jnp.where(
            low_half, image[e, 16:24, 0:HALF], pltpu.roll(image[e, 16:24, HALF:COLS], 4, 0)
        )
        return 0

    lax.fori_loop(0, EXPS, pack, 0)
    pl.semaphore_wait(barrier, len(partners))

    def halo(direction, e):
        return pltpu.make_async_remote_copy(
            src_ref=h_send.at[direction, e],
            dst_ref=h_recv.at[direction, e],
            send_sem=halo_s.at[direction, e],
            recv_sem=halo_r.at[direction, e],
            device_id=(after if direction == 0 else before, exp),
            device_id_type=MESH,
        )

    def start_halo(e, _):
        halo(0, e).start()
        halo(1, e).start()
        return 0

    lax.fori_loop(0, EXPS, start_halo, 0)

    def meta(d):
        return pltpu.make_async_remote_copy(
            src_ref=m_buf, dst_ref=m_got.at[exp], send_sem=m_s.at[d], recv_sem=m_r.at[d],
            device_id=(sky, peers[d]), device_id_type=MESH,
        )

    for d in range(1, N_EXP):
        meta(d).start()
    m_got[exp] = m_buf[...]

    load_variance.wait()

    def weights(eb, _):
        e, rb = eb // 4, lax.rem(eb, 4)
        rows = pl.ds(pl.multiple_of(rb * 8, 8), 8)
        for part in range(2):
            for q in range(N_EXP):
                lane = part * HALF + q * LANES
                w_buf[q, eb * 2 + part] = 1.0 / variance[e, rows, lane:lane + LANES]
        return 0

    lax.fori_loop(0, BLOCKS, weights, 0)

    def send_w(d):
        return pltpu.make_async_remote_copy(
            src_ref=w_buf.at[peers[d]], dst_ref=w_got.at[exp], send_sem=w_s.at[d], recv_sem=w_r.at[d],
            device_id=(sky, peers[d]), device_id_type=MESH,
        )

    for d in range(1, N_EXP):
        send_w(d).start()
    own_w = pltpu.make_async_copy(w_buf.at[exp], w_got.at[exp], own_s.at[0])
    own_w.start()

    k3 = iota((ROWS, STEP), 1)
    k = lax.rem(k3, 80)
    source = jnp.where(
        k < 32, k, jnp.where(k < 48, k - 48, jnp.where(k < 68, k - 16, jnp.where(k < 72, k - 88, 1000)))
    )
    source = jnp.where(k3 < 240, source, 1000)
    source = jnp.where((source < 0) & (sky == 0), 1000, source)
    source = jnp.where((source >= ROWS) & (sky == N_SKY - 1), 1000, source)
    row_lag = source - iota((ROWS, STEP), 0) + RIM

    def row_band(b, _):
        def tap(t, band):
            return jnp.where(row_lag == t, row_taps[b, t], band)

        v_base[b] = lax.fori_loop(0, TAPS, tap, jnp.zeros((ROWS, STEP), F32))
        return 0

    lax.fori_loop(0, NB, row_band, 0)

    h_hi[...] = jnp.zeros(h_hi.shape, BF16)
    h_lo[...] = jnp.zeros(h_lo.shape, BF16)
    col_diff = iota((LANES, LANES), 0) - iota((LANES, LANES), 1) + RIM

    def col_band(b, _):
        for shift in (-1, 0, 1):
            lag = col_diff + LANES * shift

            def tap(t, band):
                return jnp.where(lag == t, col_taps[b, t], band)

            high, low = split(lax.fori_loop(0, TAPS, tap, jnp.zeros((LANES, LANES), F32)))
            for u in range(2):
                rows = slice((u + 1 + shift) * LANES, (u + 2 + shift) * LANES)
                h_hi[b, rows, u * LANES:(u + 1) * LANES] = high
                h_lo[b, rows, u * LANES:(u + 1) * LANES] = low
        return 0

    lax.fori_loop(0, NB, col_band, 0)

    for part_z in (z_hi, z_lo):
        part_z[:, :, 0:LANES] = jnp.zeros((NB, PER * ROWS, LANES), BF16)
        part_z[:, :, LANES + COLS:] = jnp.zeros((NB, PER * ROWS, LANES), BF16)

    for d in range(1, N_EXP):
        meta(d).wait_recv()
    table = pltpu.make_async_copy(m_got, m_smem, own_s.at[1])
    table.start()
    table.wait()

    lane = iota((8, 2 * LANES), 1)
    lane_slot, lane_row = lane >> 3, lane & 7
    patch_row = iota((PR, 2 * LANES), 0)

    def select_rows(p, _):
        target = jnp.zeros((8, 2 * LANES), I32)
        for g in range(N_EXP):
            for j in range(SLOTS):
                target = jnp.where(lane_slot == g * SLOTS + j, m_smem[g, 1, p * SLOTS + j], target)
        target = (target + lane_row)[0:1]
        slots[p] = jnp.where(patch_row == target, 1.0, 0.0).astype(BF16)
        return 0

    lax.fori_loop(0, N_SKY, select_rows, 0)

    def add_strips(got, acc, p):
        tiles = [
            got[g, m_smem[g, 0, p * SLOTS + j] & (2 * BLOCKS - 1)] for g in range(N_EXP) for j in range(SLOTS)
        ]
        high, low = split(jnp.concatenate(tiles, 0))
        both = jnp.dot(slots[p], jnp.concatenate([high, low], 1), preferred_element_type=F32)
        acc[p // NX, lax.rem(p, NX)] = both[:, 0:LANES] + both[:, LANES:]

    def halves(size):
        def half(ref, which):
            return ref.at[which * size:(which + 1) * size]

        return half

    top, low_part = pl.ds(0, PR // 2), pl.ds(PR // 2, PR // 2)
    w_z = Ring(NZ, z, at_z, lambda o: acc_w.at[o], halves(NX // 2), land_wz, wz_s, wz_r)
    w_x = Ring(NX, x, at_x, lambda o: mid_w.at[o], halves(PR // 2), land_wx, wx_s, wx_r)
    a_x = Ring(NX, x, at_x, lambda o: acc_v.at[:, o, top], halves(NZ // 2), land_ax, ax_s, ax_r)
    a_z = Ring(NZ, z, at_z, lambda o: mid_a.at[o], halves(PR // 4), land_az, az_s, az_r)
    b_z = Ring(NZ, z, at_z, lambda o: acc_v.at[o, :, low_part], halves(NX // 2), land_bz, bz_s, bz_r)
    b_x = Ring(NX, x, at_x, lambda o: mid_b.at[o], halves(PR // 4), land_bx, bx_s, bx_r)

    def send_v(c, d):
        span = pl.ds(c * (8 * PER), 8 * PER)
        return pltpu.make_async_remote_copy(
            src_ref=v_buf.at[peers[d], span], dst_ref=v_got.at[exp, span],
            send_sem=v_s.at[c, d], recv_sem=v_r.at[c, d],
            device_id=(sky, peers[d]), device_id_type=MESH,
        )

    third = iota((NB * ROWS, STEP), 1) >= 160
    low_rows = iota((8, STEP), 0) < 4

    def chunk(c, _):
        @pl.when(c == CHUNKS - 1)
        def _():
            for d in range(1, N_EXP):
                send_w(d).wait_recv()
            own_w.wait()

            def add_weights(p, _):
                add_strips(w_got, acc_w, p)
                return 0

            lax.fori_loop(0, N_SKY, add_weights, 0)
            w_z.begin()

        def vertical(el, _):
            e = c * PER + el
            halo(0, e).wait_recv()
            halo(1, e).wait_recv()
            table_row = coef_index[e]
            bands = [coef_table[b, table_row] * v_base[b] for b in range(NB)]
            high, low = split(jnp.concatenate(bands, 0))
            left = jnp.where(third, low.astype(F32), high.astype(F32)).astype(BF16)
            out_rows = pl.ds(pl.multiple_of(el * ROWS, ROWS), ROWS)
            for j in range(NSTEP):
                part, at = divmod(j * STEP, HALF)
                cols = slice(at, at + STEP)
                up = h_recv[0, e, 2 * part:2 * part + 2, :, cols].reshape(16, STEP)
                down = h_recv[1, e, 2 * part:2 * part + 2, :, cols].reshape(16, STEP)
                up4, down4 = h_recv[0, e, 4, :, cols], h_recv[1, e, 4, :, cols]
                if part == 0:
                    rest = jnp.where(low_rows, down4, up4)
                else:
                    rest = pltpu.roll(jnp.where(low_rows, up4, down4), 4, 0)
                rows = jnp.concatenate(
                    [image[e, :, j * STEP:(j + 1) * STEP], up, down, rest, jnp.zeros((8, STEP), F32)], 0
                )
                x_hi, x_lo = split(rows)
                right = jnp.concatenate([x_hi, x_lo, x_hi, jnp.zeros((16, STEP), BF16)], 0)
                high_z, low_z = split(jnp.dot(left, right, preferred_element_type=F32))
                at = LANES + j * STEP
                z_hi[:, out_rows, at:at + STEP] = high_z.reshape(NB, ROWS, STEP)
                z_lo[:, out_rows, at:at + STEP] = low_z.reshape(NB, ROWS, STEP)
            return 0

        lax.fori_loop(0, PER, vertical, 0)

        def horizontal(j, _):
            cols = pl.ds(pl.multiple_of(j * STEP, STEP), 2 * STEP)
            total = jnp.zeros((PER * ROWS, STEP), F32)
            for b in range(NB):
                zh, zl = z_hi[b, :, cols], z_lo[b, :, cols]
                total += jnp.dot(zh, h_hi[b], preferred_element_type=F32)
                total += jnp.dot(zl, h_hi[b], preferred_element_type=F32)
                total += jnp.dot(zh, h_lo[b], preferred_element_type=F32)
            part = j // 4
            for u in range(2):
                q = lax.rem(j, 4) * 2 + u
                for r in range(4 * PER):
                    piece = total[r * 8:(r + 1) * 8, u * LANES:(u + 1) * LANES]
                    strip = (c * (4 * PER) + r) * 2 + part
                    v_buf[q, strip] = piece * w_buf[q, strip]
            return 0

        lax.fori_loop(0, NSTEP, horizontal, 0)
        for d in range(1, N_EXP):
            send_v(c, d).start()
        return 0

    lax.fori_loop(0, CHUNKS, chunk, 0)
    own_v = pltpu.make_async_copy(v_buf.at[exp], v_got.at[exp], own_s.at[2])
    own_v.start()

    w_z.advance(1)
    w_z.advance(2)
    w_z.advance(3)

    def arrived_v(c, _):
        for d in range(1, N_EXP):
            send_v(c, d).wait_recv()
        return 0

    lax.fori_loop(0, CHUNKS, arrived_v, 0)
    own_v.wait()

    def add_values(p, _):
        add_strips(v_got, acc_v, p)
        return 0

    lax.fori_loop(0, N_SKY, add_values, 0)
    a_x.begin()
    b_z.begin()
    mid_w[...] = w_z.total()
    w_x.begin()
    a_x.advance(1)
    b_z.advance(1)
    w_x.advance(1)
    b_z.advance(2)
    mid_a[...] = a_x.total()
    a_z.begin()
    b_z.advance(3)
    fin_w[...] = w_x.total()

    def rows_copy(fin, land, send, recv, d):
        return pltpu.make_async_remote_copy(
            src_ref=fin.at[pl.ds(pl.multiple_of(peers[d] * 16, 16), 16)],
            dst_ref=land.at[exp],
            send_sem=send.at[d], recv_sem=recv.at[d],
            device_id=(sky, peers[d]), device_id_type=MESH,
        )

    mine = pl.ds(pl.multiple_of(exp * 16, 16), 16)
    for d in range(1, N_EXP):
        rows_copy(fin_w, rows_w, rw_s, rw_r, d).start()
    rows_w[exp] = fin_w[mine]
    a_z.advance(1)
    mid_b[...] = b_z.total()
    b_x.begin()
    a_z.advance(2)
    b_x.advance(1)
    a_z.advance(3)
    fin_v[PR // 2:] = b_x.total()
    fin_v[:PR // 2] = a_z.total()
    for d in range(1, N_EXP):
        rows_copy(fin_v, rows_v, rv_s, rv_r, d).start()
    rows_v[exp] = fin_v[mine]
    for d in range(1, N_EXP):
        rows_copy(fin_w, rows_w, rw_s, rw_r, d).wait()
    for q in range(N_EXP):
        out[1, :, q * LANES:(q + 1) * LANES] = rows_w[q]

    def end_halo(e, _):
        halo(0, e).wait_send()
        halo(1, e).wait_send()
        return 0

    lax.fori_loop(0, EXPS, end_halo, 0)
    for d in range(1, N_EXP):
        meta(d).wait_send()
        send_w(d).wait_send()

    def end_v(c, _):
        for d in range(1, N_EXP):
            send_v(c, d).wait_send()
        return 0

    lax.fori_loop(0, CHUNKS, end_v, 0)
    for ring in (w_z, w_x, a_x, a_z, b_z, b_x):
        ring.drain()
    for d in range(1, N_EXP):
        rows_copy(fin_v, rows_v, rv_s, rv_r, d).wait()
    for q in range(N_EXP):
        out[0, :, q * LANES:(q + 1) * LANES] = rows_v[q]


def per_device(image, variance, coef_index, coef_table, row_taps, col_taps, destination, offset):
    vmem, smem, anywhere = (pl.BlockSpec(memory_space=s) for s in (pltpu.VMEM, pltpu.SMEM, pl.ANY))
    dma = pltpu.SemaphoreType.DMA

    def held(*shape, dtype=F32):
        return pltpu.VMEM(shape, dtype)

    strips = (N_EXP, 2 * BLOCKS, 8, LANES)
    sums = pl.pallas_call(
        coadd_kernel,
        out_shape=jax.ShapeDtypeStruct((2, PR // N_EXP, HALF), F32),
        in_specs=[anywhere] * 2 + [vmem] * 2 + [smem] * 4,
        out_specs=vmem,
        scratch_shapes=[
            held(EXPS, ROWS, COLS), held(EXPS, ROWS, COLS),
            held(2, EXPS, 5, 8, HALF), held(2, EXPS, 5, 8, HALF),
            held(*strips), held(*strips), held(*strips), held(*strips),
            held(8, LANES, dtype=I32), held(N_EXP, 8, LANES, dtype=I32),
            pltpu.SMEM((N_EXP, 8, LANES), I32),
            held(N_SKY, PR, 2 * LANES, dtype=BF16),
            held(NB, PER * ROWS, COLS + 2 * LANES, dtype=BF16),
            held(NB, PER * ROWS, COLS + 2 * LANES, dtype=BF16),
            held(NB, 2 * STEP, STEP, dtype=BF16),
            held(NB, 2 * STEP, STEP, dtype=BF16),
            held(NB, ROWS, STEP),
            held(NZ, NX, PR, LANES), held(NZ, NX, PR, LANES),
            held(2, 4, NX, PR, LANES), held(2, 2, PR, LANES),
            held(2, 2, NZ, PR // 2, LANES), held(2, 4, PR // 2, LANES),
            held(2, 4, NX, PR // 2, LANES), held(2, 2, PR // 2, LANES),
            held(NX, PR, LANES), held(NZ, PR // 2, LANES), held(NX, PR // 2, LANES),
            held(PR, LANES), held(PR, LANES),
            held(N_EXP, PR // N_EXP, LANES), held(N_EXP, PR // N_EXP, LANES),
            dma((2,)), dma((2, EXPS)), dma((2, EXPS)),
            dma((N_EXP,)), dma((N_EXP,)),
            dma((CHUNKS, N_EXP)), dma((CHUNKS, N_EXP)),
            dma((N_EXP,)), dma((N_EXP,)),
            dma((3,)),
        ] + [dma((2, n)) for n in (5, 5, 3, 3, 3, 3, 5, 5, 5, 5, 3, 3)] + [dma((N_EXP,))] * 4,
        compiler_params=pltpu.CompilerParams(
            collective_id=0, has_side_effects=True, vmem_limit_bytes=60 * 1024 * 1024
        ),
    )(
        image, variance, destination.reshape(1, -1), offset.reshape(1, -1),
        coef_index, coef_table.T, row_taps, col_taps,
    )
    return sums[0] / (1.0 + sums[1]), sums[1]


def solution(mesh):
    placed = (
        P("exp", "sky", None),
        P("exp", "sky", None),
        P("exp"),
        P(),
        P(),
        P(),
        P("exp", "sky", None, None),
        P("exp", "sky", None),
    )
    return jax.shard_map(
        per_device,
        mesh=mesh,
        in_specs=placed,
        out_specs=(P(("sky", "exp"), None), P(("sky", "exp"), None)),
        check_vma=False,
    )
```

```python
import jax
import jax.numpy as jnp
from jax import lax
from jax.experimental import pallas as pl
from jax.experimental.pallas import tpu as pltpu
from jax.sharding import PartitionSpec as P

MESH = pl.DeviceIdType.MESH
F32, BF16, I32 = jnp.float32, jnp.bfloat16, jnp.int32

NB, TAPS, RIM = 5, 41, 20
N_SKY, N_EXP, NX, NZ = 32, 8, 4, 8
EXPS, ROWS, COLS, HALF = 8, 32, 2048, 1024
BLOCKS = EXPS * ROWS // 8
LANES = 128
PR, PATCH_ROWS = 128, 4096
SEND = 2
CHUNKS = EXPS // SEND
SLOTS_AT = 3
WEIGHTS_AT = 6
STEP = 256
NSTEP = COLS // STEP


def iota(shape, dim):
    return lax.broadcasted_iota(I32, shape, dim)


def greet(devices):
    barrier = pltpu.get_barrier_semaphore()
    for device in devices:
        pl.semaphore_signal(barrier, inc=1, device_id=device, device_id_type=MESH)
    pl.semaphore_wait(barrier, len(devices))


def split(value):
    high = value.astype(BF16)
    return high, (value - high.astype(F32)).astype(BF16)

SLOTS = 4
EMPTY = -4096


def strip_table(dest, offs):
    sub, lane = iota((64, LANES), 0), iota((64, LANES), 1)
    line = jnp.concatenate([dest, jnp.full((1, 64), -1, I32)], 1)
    shift = jnp.concatenate([offs, jnp.zeros((1, 64), I32)], 1)
    diagonal = sub == lane
    patch = jnp.sum(jnp.where(diagonal, line, 0), 1, keepdims=True)
    first = jnp.sum(jnp.where(diagonal, shift, 0), 1, keepdims=True)
    rank = jnp.sum(jnp.where((patch == line) & (lane < sub), 1, 0), 1, keepdims=True)
    here = patch * SLOTS + rank == lane
    strip = jnp.sum(jnp.where(here, sub, 0), 0, keepdims=True)
    start = jnp.sum(jnp.where(here, first - EMPTY, 0), 0, keepdims=True) + EMPTY
    row = iota((8, LANES), 0)
    return jnp.where(row == 0, strip, jnp.where(row == 1, start, 0))


class Ring:
    def __init__(self, size, me, target, chunk, half, land, send, recv):
        self.size, self.me, self.target = size, me, target
        self.chunk, self.half, self.land = chunk, half, land
        self.send, self.recv = send, recv
        self.steps = size // 2

    def owner(self, way, distance):
        return lax.rem(self.me + (distance if way == 0 else self.size - distance), self.size)

    def copy(self, src, dst, way, number):
        return pltpu.make_async_remote_copy(
            src_ref=src, dst_ref=dst, send_sem=self.send.at[way, number], recv_sem=self.recv.at[way, number],
            device_id=self.target(self.owner(way, 1)), device_id_type=MESH,
        )

    def copies(self, way, step):
        own = self.chunk(self.owner(way, self.steps - step))
        here = self.land.at[way, step]
        if step == 0:
            return [self.copy(self.half(own, way), self.half(here, way), way, 0)], []
        came = self.land.at[way, step - 1]
        if step == 1:
            early = [self.copy(self.half(own, 1 - way), self.half(here, 1 - way), way, 1)]
            return early, [self.copy(self.half(came, way), self.half(here, way), way, 2)]
        return [], [self.copy(came, here, way, step + 1)]

    def begin(self, *steps):
        for step in steps or (0, 1):
            for way in (0, 1):
                for copy in self.copies(way, step)[0]:
                    copy.start()

    def arrived(self, way, step):
        early, late = self.copies(way, step)
        for copy in early + late:
            copy.wait_recv()

    def advance(self, step):
        for way in (0, 1):
            self.arrived(way, step - 1)
            came = self.land.at[way, step - 1]
            own = self.chunk(self.owner(way, self.steps - step))
            if step == 1:
                came, own = self.half(came, way), self.half(own, way)
            came[...] = came[...] + own[...]
            for copy in self.copies(way, step)[1]:
                copy.start()

    def total(self):
        last = self.steps - 1
        for way in (0, 1):
            self.arrived(way, last)
        return self.chunk(self.me)[...] + self.land[0, last] + self.land[1, last]

    def drain(self):
        for step in range(self.steps):
            for way in (0, 1):
                early, late = self.copies(way, step)
                for copy in early + late:
                    copy.wait_send()


class Direct:
    def __init__(self, size, me, target, chunk, land, send, recv):
        self.size, self.me, self.target = size, me, target
        self.chunk, self.land, self.send, self.recv = chunk, land, send, recv

    def copy(self, d):
        owner = lax.rem(self.me + d, self.size)
        return pltpu.make_async_remote_copy(
            src_ref=self.chunk(owner), dst_ref=self.land.at[d], send_sem=self.send.at[d], recv_sem=self.recv.at[d],
            device_id=self.target(owner), device_id_type=MESH,
        )

    def begin(self):
        for d in range(1, self.size):
            self.copy(d).start()

    def total(self):
        total = self.chunk(self.me)[...]
        for d in range(1, self.size):
            self.copy(d).wait_recv()
            total = total + self.land[d]
        return total

    def drain(self):
        for d in range(1, self.size):
            self.copy(d).wait_send()


def coadd_kernel(
    image_in, variance_in, dest, offs, coef_index, coef_table, row_taps, col_taps,
    out,
    image, variance, h_send, h_recv, w_buf, v_buf, w_got, v_got, m_buf, m_got, m_smem, slots,
    z_hi, z_lo, h_all, v_base, acc_w, acc_v,
    land_ua, land_uaz, land_ub, land_ubx, land_a, land_az, land_b, land_bx, mid_ua, mid_ub, mid_a, mid_b, fin_w, fin_v, rows_w, rows_v,
    load_s, halo_s, halo_r, w_s, w_r, v_s, v_r, m_s, m_r, own_s,
    ua_s, ua_r, uaz_s, uaz_r, ub_s, ub_r, ubx_s, ubx_r, ax_s, ax_r, az_s, az_r, bz_s, bz_r, bx_s, bx_r, rw_s, rw_r, rv_s, rv_r,
):
    sky, exp = lax.axis_index("sky"), lax.axis_index("exp")
    z, x = sky // NX, lax.rem(sky, NX)
    after, before = lax.rem(sky + 1, N_SKY), lax.rem(sky + N_SKY - 1, N_SKY)
    peers = [lax.rem(exp + d, N_EXP) for d in range(N_EXP)]

    def at_x(other):
        return (z * NX + other, exp)

    def at_z(other):
        return (other * NX + x, exp)

    load_image = pltpu.make_async_copy(image_in, image, load_s.at[0])
    load_variance = pltpu.make_async_copy(variance_in, variance, load_s.at[1])
    load_variance.start()
    load_image.start()

    partners = [(after, exp), (before, exp)] + [(sky, q) for q in peers[1:]] + [
        at_x(lax.rem(x + d, NX)) for d in range(1, NX)
    ] + [at_z(lax.rem(z + d, NZ)) for d in range(1, NZ)]
    barrier = pltpu.get_barrier_semaphore()
    for device in partners:
        pl.semaphore_signal(barrier, inc=1, device_id=device, device_id_type=MESH)

    load_variance.wait()

    def weights(eb, _):
        e, rb = eb // 4, lax.rem(eb, 4)
        rows = pl.ds(pl.multiple_of(rb * 8, 8), 8)
        for part in range(2):
            for q in range(N_EXP):
                lane = part * HALF + q * LANES
                w_buf[q, eb * 2 + part] = 1.0 / variance[e, rows, lane:lane + LANES]
        return 0

    lax.fori_loop(0, BLOCKS, weights, 0)
    load_image.wait()
    low_half = iota((8, HALF), 0) < 4

    def pack(e, _):
        h_send[0, e, 0] = image[e, 16:24, 0:HALF]
        h_send[0, e, 1] = image[e, 24:32, 0:HALF]
        h_send[0, e, 2] = image[e, 16:24, HALF:COLS]
        h_send[0, e, 3] = image[e, 24:32, HALF:COLS]
        h_send[0, e, 4] = jnp.where(
            low_half, pltpu.roll(image[e, 8:16, HALF:COLS], 4, 0), image[e, 8:16, 0:HALF]
        )
        h_send[1, e, 0] = image[e, 0:8, 0:HALF]
        h_send[1, e, 1] = image[e, 8:16, 0:HALF]
        h_send[1, e, 2] = image[e, 0:8, HALF:COLS]
        h_send[1, e, 3] = image[e, 8:16, HALF:COLS]
        h_send[1, e, 4] = jnp.where(
            low_half, image[e, 16:24, 0:HALF], pltpu.roll(image[e, 16:24, HALF:COLS], 4, 0)
        )
        return 0

    lax.fori_loop(0, EXPS, pack, 0)
    m_buf[...] = strip_table(dest[...], offs[...])
    pl.semaphore_wait(barrier, len(partners))

    def halo(direction, e):
        return pltpu.make_async_remote_copy(
            src_ref=h_send.at[direction, e],
            dst_ref=h_recv.at[direction, e],
            send_sem=halo_s.at[direction, e],
            recv_sem=halo_r.at[direction, e],
            device_id=(after if direction == 0 else before, exp),
            device_id_type=MESH,
        )

    def meta(d):
        return pltpu.make_async_remote_copy(
            src_ref=m_buf, dst_ref=m_got.at[exp], send_sem=m_s.at[d], recv_sem=m_r.at[d],
            device_id=(sky, peers[d]), device_id_type=MESH,
        )

    def send_w(c, d):
        span = pl.ds(c * (8 * SEND), 8 * SEND)
        return pltpu.make_async_remote_copy(
            src_ref=w_buf.at[peers[d], span], dst_ref=w_got.at[exp, span],
            send_sem=w_s.at[c, d], recv_sem=w_r.at[c, d],
            device_id=(sky, peers[d]), device_id_type=MESH,
        )

    for d in range(1, N_EXP):
        meta(d).start()
    m_got[exp] = m_buf[...]

    def start_sends(c, _):
        for i in range(SEND):
            halo(0, c * SEND + i).start()
            halo(1, c * SEND + i).start()
        for d in range(1, N_EXP):
            send_w(c, d).start()
        return 0

    lax.fori_loop(0, CHUNKS, start_sends, 0)
    own_w = pltpu.make_async_copy(w_buf.at[exp], w_got.at[exp], own_s.at[0])
    own_w.start()

    k3 = iota((ROWS, STEP), 1)
    k = lax.rem(k3, 80)
    source = jnp.where(
        k < 32, k, jnp.where(k < 48, k - 48, jnp.where(k < 68, k - 16, jnp.where(k < 72, k - 88, 1000)))
    )
    source = jnp.where(k3 < 240, source, 1000)
    source = jnp.where((source < 0) & (sky == 0), 1000, source)
    source = jnp.where((source >= ROWS) & (sky == N_SKY - 1), 1000, source)
    row_lag = source - iota((ROWS, STEP), 0) + RIM

    def row_band(b, _):
        def tap(t, band):
            return jnp.where(row_lag == t, row_taps[b, t], band)

        v_base[b] = lax.fori_loop(0, TAPS, tap, jnp.zeros((ROWS, STEP), F32))
        return 0

    lax.fori_loop(0, NB, row_band, 0)

    h_all[...] = jnp.zeros(h_all.shape, BF16)
    col_diff = iota((LANES, LANES), 0) - iota((LANES, LANES), 1) + RIM

    def col_band(b, _):
        for shift in (-1, 0, 1):
            lag = col_diff + LANES * shift

            def tap(t, band):
                return jnp.where(lag == t, col_taps[b, t], band)

            high, low = split(lax.fori_loop(0, TAPS, tap, jnp.zeros((LANES, LANES), F32)))
            for u in range(2):
                for third, band in enumerate((high, high, low)):
                    row = third * 2 * STEP + (u + 1 + shift) * LANES
                    h_all[b, row:row + LANES, u * LANES:(u + 1) * LANES] = band
        return 0

    lax.fori_loop(0, NB, col_band, 0)

    for part_z in (z_hi, z_lo):
        part_z[:, :, 0:LANES] = jnp.zeros((NB, ROWS, LANES), BF16)
        part_z[:, :, LANES + COLS:] = jnp.zeros((NB, ROWS, LANES), BF16)

    lane = iota((8, 2 * LANES), 1)
    lane_slot, lane_row = lane >> 3, lane & 7
    patch_row = iota((PR, 2 * LANES), 0)

    def select_rows(p, _):
        target = jnp.zeros((8, 2 * LANES), I32)
        for g in range(N_EXP):
            for j in range(SLOTS):
                target = jnp.where(lane_slot == g * SLOTS + j, m_smem[g, 1, p * SLOTS + j], target)
        target = (target + lane_row)[0:1]
        slots[p] = jnp.where(patch_row == target, 1.0, 0.0).astype(BF16)
        return 0


    def add_strips(got, acc, p):
        tiles = [
            got[g, m_smem[g, 0, p * SLOTS + j] & (2 * BLOCKS - 1)] for g in range(N_EXP) for j in range(SLOTS)
        ]
        high, low = split(jnp.concatenate(tiles, 0))
        both = jnp.dot(slots[p], jnp.concatenate([high, low], 1), preferred_element_type=F32)
        acc[p // NX, lax.rem(p, NX)] = both[:, 0:LANES] + both[:, LANES:]

    def halves(size):
        def half(ref, which):
            return ref.at[which * size:(which + 1) * size]

        return half

    def sums(acc, rows, x_first, land, land2, mid, send, recv, send2, recv2):
        if x_first:
            ring = Ring(NX, x, at_x, lambda o: acc.at[:, o, rows], halves(NZ // 2), land, send, recv)
            return ring, Direct(NZ, z, at_z, lambda o: mid.at[o], land2, send2, recv2)
        ring = Ring(NZ, z, at_z, lambda o: acc.at[o, :, rows], halves(NX // 2), land, send, recv)
        return ring, Direct(NX, x, at_x, lambda o: mid.at[o], land2, send2, recv2)

    u_a, u_az = sums(acc_w, pl.ds(0, 64), True, land_ua, land_uaz, mid_ua, ua_s, ua_r, uaz_s, uaz_r)
    u_b, u_bx = sums(acc_w, pl.ds(64, 64), False, land_ub, land_ubx, mid_ub, ub_s, ub_r, ubx_s, ubx_r)
    a_x, a_z, b_z, b_x = [], [], [], []
    for i in range(2):
        first, second = sums(
            acc_v, pl.ds(i * 32, 32), True, land_a.at[i], land_az.at[i], mid_a.at[i],
            ax_s.at[i], ax_r.at[i], az_s.at[i], az_r.at[i],
        )
        a_x.append(first)
        a_z.append(second)
        first, second = sums(
            acc_v, pl.ds(64 + i * 32, 32), False, land_b.at[i], land_bx.at[i], mid_b.at[i],
            bz_s.at[i], bz_r.at[i], bx_s.at[i], bx_r.at[i],
        )
        b_z.append(first)
        b_x.append(second)

    def send_v(c, d):
        span = pl.ds(c * (8 * SEND), 8 * SEND)
        return pltpu.make_async_remote_copy(
            src_ref=v_buf.at[peers[d], span], dst_ref=v_got.at[exp, span],
            send_sem=v_s.at[c, d], recv_sem=v_r.at[c, d],
            device_id=(sky, peers[d]), device_id_type=MESH,
        )

    third = iota((NB * ROWS, STEP), 1) >= 160
    low_rows = iota((8, STEP), 0) < 4

    def exposure(e, _):
        @pl.when(e == SLOTS_AT)
        def _():
            for d in range(1, N_EXP):
                meta(d).wait_recv()
            table = pltpu.make_async_copy(m_got, m_smem, own_s.at[1])
            table.start()
            table.wait()
            lax.fori_loop(0, N_SKY, select_rows, 0)

        @pl.when(e == WEIGHTS_AT)
        def _():
            def arrived_w(c, _):
                for d in range(1, N_EXP):
                    send_w(c, d).wait_recv()
                return 0

            lax.fori_loop(0, CHUNKS, arrived_w, 0)
            own_w.wait()

            def add_weights(p, _):
                add_strips(w_got, acc_w, p)
                return 0

            lax.fori_loop(0, N_SKY, add_weights, 0, unroll=4)
            u_b.begin()
            u_a.begin()

        halo(0, e).wait_recv()
        halo(1, e).wait_recv()
        table_row = coef_index[e]
        bands = [coef_table[b, table_row] * v_base[b] for b in range(NB)]
        high, low = split(jnp.concatenate(bands, 0))
        left = jnp.where(third, low.astype(F32), high.astype(F32)).astype(BF16)
        for j in range(NSTEP):
            part, at = divmod(j * STEP, HALF)
            cols = slice(at, at + STEP)
            up = h_recv[0, e, 2 * part:2 * part + 2, :, cols].reshape(16, STEP)
            down = h_recv[1, e, 2 * part:2 * part + 2, :, cols].reshape(16, STEP)
            up4, down4 = h_recv[0, e, 4, :, cols], h_recv[1, e, 4, :, cols]
            if part == 0:
                rest = jnp.where(low_rows, down4, up4)
            else:
                rest = pltpu.roll(jnp.where(low_rows, up4, down4), 4, 0)
            rows = jnp.concatenate(
                [image[e, :, j * STEP:(j + 1) * STEP], up, down, rest, jnp.zeros((8, STEP), F32)], 0
            )
            x_hi, x_lo = split(rows)
            right = jnp.concatenate([x_hi, x_lo, x_hi, jnp.zeros((16, STEP), BF16)], 0)
            high_z, low_z = split(jnp.dot(left, right, preferred_element_type=F32))
            at = LANES + j * STEP
            z_hi[:, :, at:at + STEP] = high_z.reshape(NB, ROWS, STEP)
            z_lo[:, :, at:at + STEP] = low_z.reshape(NB, ROWS, STEP)

        total = jnp.zeros((NSTEP * ROWS, STEP), F32)
        for b in range(NB):
            highs = jnp.concatenate([z_hi[b, :, j * STEP:(j + 2) * STEP] for j in range(NSTEP)], 0)
            lows = jnp.concatenate([z_lo[b, :, j * STEP:(j + 2) * STEP] for j in range(NSTEP)], 0)
            total += jnp.dot(jnp.concatenate([highs, lows, highs], 1), h_all[b], preferred_element_type=F32)
        for j in range(NSTEP):
            part = j // 4
            for u in range(2):
                q = (j % 4) * 2 + u
                for r in range(4):
                    row = j * ROWS + r * 8
                    strip = (e * 4 + r) * 2 + part
                    v_buf[q, strip] = total[row:row + 8, u * LANES:(u + 1) * LANES] * w_buf[q, strip]

        @pl.when(lax.rem(e, SEND) == SEND - 1)
        def _():
            for d in range(1, N_EXP):
                send_v(e // SEND, d).start()

        return 0

    lax.fori_loop(0, EXPS, exposure, 0)
    own_v = pltpu.make_async_copy(v_buf.at[exp], v_got.at[exp], own_s.at[2])
    own_v.start()

    u_b.advance(1)
    u_a.advance(1)
    u_b.advance(2)
    mid_ua[...] = u_a.total()
    u_az.begin()
    u_b.advance(3)
    mid_ub[...] = u_b.total()
    u_bx.begin()

    def arrived_v(c, _):
        for d in range(1, N_EXP):
            send_v(c, d).wait_recv()
        return 0

    lax.fori_loop(0, CHUNKS, arrived_v, 0)
    own_v.wait()

    def add_values(distance):
        owner = lax.rem(z + distance, NZ)

        def add(px, _):
            add_strips(v_got, acc_v, owner * NX + px)
            return 0

        lax.fori_loop(0, NX, add, 0, unroll=True)

    add_values(4)
    for ring in b_z:
        ring.begin(0)
    add_values(3)
    add_values(5)
    for ring in b_z:
        ring.begin(1)
    for distance in (2, 6, 1, 7, 0):
        add_values(distance)
    for ring in a_x:
        ring.begin()
    fin_w[0:64] = u_az.total()
    fin_w[64:128] = u_bx.total()

    def rows_copy(fin, land, send, recv, d):
        return pltpu.make_async_remote_copy(
            src_ref=fin.at[pl.ds(pl.multiple_of(peers[d] * 16, 16), 16)],
            dst_ref=land.at[exp],
            send_sem=send.at[d], recv_sem=recv.at[d],
            device_id=(sky, peers[d]), device_id_type=MESH,
        )

    mine = pl.ds(pl.multiple_of(exp * 16, 16), 16)
    for d in range(1, N_EXP):
        rows_copy(fin_w, rows_w, rw_s, rw_r, d).start()
    rows_w[exp] = fin_w[mine]
    for ring in b_z:
        ring.advance(1)
    for ring in a_x:
        ring.advance(1)
    for ring in b_z:
        ring.advance(2)
    for i in range(2):
        mid_a[i] = a_x[i].total()
        a_z[i].begin()
    for ring in b_z:
        ring.advance(3)
    for i in range(2):
        mid_b[i] = b_z[i].total()
        b_x[i].begin()
    for i in range(2):
        fin_v[i * 32:(i + 1) * 32] = a_z[i].total()
    for i in range(2):
        fin_v[64 + i * 32:96 + i * 32] = b_x[i].total()
    for d in range(1, N_EXP):
        rows_copy(fin_v, rows_v, rv_s, rv_r, d).start()
    rows_v[exp] = fin_v[mine]
    for d in range(1, N_EXP):
        rows_copy(fin_w, rows_w, rw_s, rw_r, d).wait()
    for q in range(N_EXP):
        out[1, :, q * LANES:(q + 1) * LANES] = rows_w[q]

    def end_halo(e, _):
        halo(0, e).wait_send()
        halo(1, e).wait_send()
        return 0

    lax.fori_loop(0, EXPS, end_halo, 0)
    for d in range(1, N_EXP):
        meta(d).wait_send()

    def end_v(c, _):
        for d in range(1, N_EXP):
            send_w(c, d).wait_send()
            send_v(c, d).wait_send()
        return 0

    lax.fori_loop(0, CHUNKS, end_v, 0)
    for ring in (u_a, u_az, u_b, u_bx, *a_x, *a_z, *b_z, *b_x):
        ring.drain()
    for d in range(1, N_EXP):
        rows_copy(fin_v, rows_v, rv_s, rv_r, d).wait()
    for q in range(N_EXP):
        out[0, :, q * LANES:(q + 1) * LANES] = rows_v[q]


def per_device(image, variance, coef_index, coef_table, row_taps, col_taps, destination, offset):
    vmem, smem, anywhere = (pl.BlockSpec(memory_space=s) for s in (pltpu.VMEM, pltpu.SMEM, pl.ANY))
    dma = pltpu.SemaphoreType.DMA

    def held(*shape, dtype=F32):
        return pltpu.VMEM(shape, dtype)

    strips = (N_EXP, 2 * BLOCKS, 8, LANES)
    sums = pl.pallas_call(
        coadd_kernel,
        out_shape=jax.ShapeDtypeStruct((2, PR // N_EXP, HALF), F32),
        in_specs=[anywhere] * 2 + [vmem] * 2 + [smem] * 4,
        out_specs=vmem,
        scratch_shapes=[
            held(EXPS, ROWS, COLS), held(EXPS, ROWS, COLS),
            held(2, EXPS, 5, 8, HALF), held(2, EXPS, 5, 8, HALF),
            held(*strips), held(*strips), held(*strips), held(*strips),
            held(8, LANES, dtype=I32), held(N_EXP, 8, LANES, dtype=I32),
            pltpu.SMEM((N_EXP, 8, LANES), I32),
            held(N_SKY, PR, 2 * LANES, dtype=BF16),
            held(NB, ROWS, COLS + 2 * LANES, dtype=BF16),
            held(NB, ROWS, COLS + 2 * LANES, dtype=BF16),
            held(NB, 6 * STEP, STEP, dtype=BF16),
            held(NB, ROWS, STEP),
            held(NZ, NX, PR, LANES), held(NZ, NX, PR, LANES),
            held(2, 2, NZ, 64, LANES), held(NZ, 64, LANES),
            held(2, 4, NX, 64, LANES), held(NX, 64, LANES),
            held(2, 2, 2, NZ, 32, LANES), held(2, NZ, 32, LANES),
            held(2, 2, 4, NX, 32, LANES), held(2, NX, 32, LANES),
            held(NZ, 64, LANES), held(NX, 64, LANES), held(2, NZ, 32, LANES), held(2, NX, 32, LANES),
            held(PR, LANES), held(PR, LANES),
            held(N_EXP, PR // N_EXP, LANES), held(N_EXP, PR // N_EXP, LANES),
            dma((2,)), dma((2, EXPS)), dma((2, EXPS)),
            dma((CHUNKS, N_EXP)), dma((CHUNKS, N_EXP)),
            dma((CHUNKS, N_EXP)), dma((CHUNKS, N_EXP)),
            dma((N_EXP,)), dma((N_EXP,)),
            dma((3,)),
        ] + [
            dma(shape)
            for shape in ((2, 3), (NZ,), (2, 5), (NX,), (2, 2, 3), (2, NZ), (2, 2, 5), (2, NX), (N_EXP,), (N_EXP,))
            for _ in range(2)
        ],
        compiler_params=pltpu.CompilerParams(
            collective_id=0, has_side_effects=True, vmem_limit_bytes=60 * 1024 * 1024
        ),
    )(
        image, variance, destination.reshape(1, -1), offset.reshape(1, -1),
        coef_index, coef_table.T, row_taps, col_taps,
    )
    return sums[0] / (1.0 + sums[1]), sums[1]


def solution(mesh):
    placed = (
        P("exp", "sky", None),
        P("exp", "sky", None),
        P("exp"),
        P(),
        P(),
        P(),
        P("exp", "sky", None, None),
        P("exp", "sky", None),
    )
    return jax.shard_map(
        per_device,
        mesh=mesh,
        in_specs=placed,
        out_specs=(P(("sky", "exp"), None), P(("sky", "exp"), None)),
        check_vma=False,
    )
```

```python
import jax
import jax.numpy as jnp
from jax import lax
from jax.experimental import pallas as pl
from jax.experimental.pallas import tpu as pltpu
from jax.sharding import PartitionSpec as P

MESH = pl.DeviceIdType.MESH
F32, BF16, I32 = jnp.float32, jnp.bfloat16, jnp.int32

NB, TAPS, RIM = 5, 41, 20
N_SKY, N_EXP, NX, NZ = 32, 8, 4, 8
EXPS, ROWS, COLS, HALF = 8, 32, 2048, 1024
BLOCKS = EXPS * ROWS // 8
LANES = 128
PR, PATCH_ROWS = 128, 4096
SEND = 4
CHUNKS = EXPS // SEND
SLOTS_AT = 3
WEIGHTS_AT = 6
A_PARTS, A_ROWS = 1, 64
B_PARTS, B_ROWS = 1, 64
STEP = 256
NSTEP = COLS // STEP


def iota(shape, dim):
    return lax.broadcasted_iota(I32, shape, dim)


def greet(devices):
    barrier = pltpu.get_barrier_semaphore()
    for device in devices:
        pl.semaphore_signal(barrier, inc=1, device_id=device, device_id_type=MESH)
    pl.semaphore_wait(barrier, len(devices))


def split(value):
    high = value.astype(BF16)
    return high, (value - high.astype(F32)).astype(BF16)

SLOTS = 4
EMPTY = -4096


def strip_table(dest, offs):
    sub, lane = iota((64, LANES), 0), iota((64, LANES), 1)
    line = jnp.concatenate([dest, jnp.full((1, 64), -1, I32)], 1)
    shift = jnp.concatenate([offs, jnp.zeros((1, 64), I32)], 1)
    diagonal = sub == lane
    patch = jnp.sum(jnp.where(diagonal, line, 0), 1, keepdims=True)
    first = jnp.sum(jnp.where(diagonal, shift, 0), 1, keepdims=True)
    rank = jnp.sum(jnp.where((patch == line) & (lane < sub), 1, 0), 1, keepdims=True)
    here = patch * SLOTS + rank == lane
    strip = jnp.sum(jnp.where(here, sub, 0), 0, keepdims=True)
    start = jnp.sum(jnp.where(here, first - EMPTY, 0), 0, keepdims=True) + EMPTY
    row = iota((8, LANES), 0)
    return jnp.where(row == 0, strip, jnp.where(row == 1, start, 0))


class Ring:
    def __init__(self, size, me, target, chunk, half, land, send, recv):
        self.size, self.me, self.target = size, me, target
        self.chunk, self.half, self.land = chunk, half, land
        self.send, self.recv = send, recv
        self.steps = size // 2

    def owner(self, way, distance):
        return lax.rem(self.me + (distance if way == 0 else self.size - distance), self.size)

    def copy(self, src, dst, way, number):
        return pltpu.make_async_remote_copy(
            src_ref=src, dst_ref=dst, send_sem=self.send.at[way, number], recv_sem=self.recv.at[way, number],
            device_id=self.target(self.owner(way, 1)), device_id_type=MESH,
        )

    def copies(self, way, step):
        own = self.chunk(self.owner(way, self.steps - step))
        here = self.land.at[way, step]
        if step == 0:
            return [self.copy(self.half(own, way), self.half(here, way), way, 0)], []
        came = self.land.at[way, step - 1]
        if step == 1:
            early = [self.copy(self.half(own, 1 - way), self.half(here, 1 - way), way, 1)]
            return early, [self.copy(self.half(came, way), self.half(here, way), way, 2)]
        return [], [self.copy(came, here, way, step + 1)]

    def begin(self, *steps):
        for step in steps or (0, 1):
            for way in (0, 1):
                for copy in self.copies(way, step)[0]:
                    copy.start()

    def arrived(self, way, step):
        early, late = self.copies(way, step)
        for copy in early + late:
            copy.wait_recv()

    def advance(self, step):
        for way in (0, 1):
            self.arrived(way, step - 1)
            came = self.land.at[way, step - 1]
            own = self.chunk(self.owner(way, self.steps - step))
            if step == 1:
                came, own = self.half(came, way), self.half(own, way)
            came[...] = came[...] + own[...]
            for copy in self.copies(way, step)[1]:
                copy.start()

    def total(self):
        last = self.steps - 1
        for way in (0, 1):
            self.arrived(way, last)
        return self.chunk(self.me)[...] + self.land[0, last] + self.land[1, last]

    def drain(self):
        for step in range(self.steps):
            for way in (0, 1):
                early, late = self.copies(way, step)
                for copy in early + late:
                    copy.wait_send()


class Direct:
    def __init__(self, size, me, target, chunk, land, send, recv):
        self.size, self.me, self.target = size, me, target
        self.chunk, self.land, self.send, self.recv = chunk, land, send, recv

    def copy(self, d):
        owner = lax.rem(self.me + d, self.size)
        return pltpu.make_async_remote_copy(
            src_ref=self.chunk(owner), dst_ref=self.land.at[d], send_sem=self.send.at[d], recv_sem=self.recv.at[d],
            device_id=self.target(owner), device_id_type=MESH,
        )

    def begin(self):
        for d in range(1, self.size):
            self.copy(d).start()

    def total(self):
        total = self.chunk(self.me)[...]
        for d in range(1, self.size):
            self.copy(d).wait_recv()
            total = total + self.land[d]
        return total

    def drain(self):
        for d in range(1, self.size):
            self.copy(d).wait_send()


def coadd_kernel(
    image_in, variance_in, dest, offs, coef_index, coef_table, row_taps, col_taps,
    out,
    image, variance, h_send, h_recv, w_buf, v_buf, w_got, v_got, m_buf, m_got, m_smem, slots,
    z_hi, z_lo, h_all, v_base, acc_w, acc_v,
    land_ua, land_uaz, land_ub, land_ubx, land_a, land_az, land_b, land_bx, mid_ua, mid_ub, mid_a, mid_b, fin_w, fin_v, rows_w, rows_v,
    load_s, halo_s, halo_r, w_s, w_r, v_s, v_r, m_s, m_r, own_s,
    ua_s, ua_r, uaz_s, uaz_r, ub_s, ub_r, ubx_s, ubx_r, ax_s, ax_r, az_s, az_r, bz_s, bz_r, bx_s, bx_r, rw_s, rw_r, rv_s, rv_r,
):
    sky, exp = lax.axis_index("sky"), lax.axis_index("exp")
    z, x = sky // NX, lax.rem(sky, NX)
    after, before = lax.rem(sky + 1, N_SKY), lax.rem(sky + N_SKY - 1, N_SKY)
    peers = [lax.rem(exp + d, N_EXP) for d in range(N_EXP)]

    def at_x(other):
        return (z * NX + other, exp)

    def at_z(other):
        return (other * NX + x, exp)

    load_image = pltpu.make_async_copy(image_in, image, load_s.at[0])
    load_variance = pltpu.make_async_copy(variance_in, variance, load_s.at[1])
    load_variance.start()
    load_image.start()

    partners = [(after, exp), (before, exp)] + [(sky, q) for q in peers[1:]] + [
        at_x(lax.rem(x + d, NX)) for d in range(1, NX)
    ] + [at_z(lax.rem(z + d, NZ)) for d in range(1, NZ)]
    barrier = pltpu.get_barrier_semaphore()
    for device in partners:
        pl.semaphore_signal(barrier, inc=1, device_id=device, device_id_type=MESH)

    load_variance.wait()

    def weights(eb, _):
        e, rb = eb // 4, lax.rem(eb, 4)
        rows = pl.ds(pl.multiple_of(rb * 8, 8), 8)
        for part in range(2):
            for q in range(N_EXP):
                lane = part * HALF + q * LANES
                w_buf[q, eb * 2 + part] = 1.0 / variance[e, rows, lane:lane + LANES]
        return 0

    lax.fori_loop(0, BLOCKS, weights, 0)
    load_image.wait()
    low_half = iota((8, HALF), 0) < 4

    def pack(e, _):
        h_send[0, e, 0] = image[e, 16:24, 0:HALF]
        h_send[0, e, 1] = image[e, 24:32, 0:HALF]
        h_send[0, e, 2] = image[e, 16:24, HALF:COLS]
        h_send[0, e, 3] = image[e, 24:32, HALF:COLS]
        h_send[0, e, 4] = jnp.where(
            low_half, pltpu.roll(image[e, 8:16, HALF:COLS], 4, 0), image[e, 8:16, 0:HALF]
        )
        h_send[1, e, 0] = image[e, 0:8, 0:HALF]
        h_send[1, e, 1] = image[e, 8:16, 0:HALF]
        h_send[1, e, 2] = image[e, 0:8, HALF:COLS]
        h_send[1, e, 3] = image[e, 8:16, HALF:COLS]
        h_send[1, e, 4] = jnp.where(
            low_half, image[e, 16:24, 0:HALF], pltpu.roll(image[e, 16:24, HALF:COLS], 4, 0)
        )
        return 0

    lax.fori_loop(0, EXPS, pack, 0)
    m_buf[...] = strip_table(dest[...], offs[...])
    pl.semaphore_wait(barrier, len(partners))

    def halo(direction, e):
        return pltpu.make_async_remote_copy(
            src_ref=h_send.at[direction, e],
            dst_ref=h_recv.at[direction, e],
            send_sem=halo_s.at[direction, e],
            recv_sem=halo_r.at[direction, e],
            device_id=(after if direction == 0 else before, exp),
            device_id_type=MESH,
        )

    def meta(d):
        return pltpu.make_async_remote_copy(
            src_ref=m_buf, dst_ref=m_got.at[exp], send_sem=m_s.at[d], recv_sem=m_r.at[d],
            device_id=(sky, peers[d]), device_id_type=MESH,
        )

    def send_w(d):
        return pltpu.make_async_remote_copy(
            src_ref=w_buf.at[peers[d]], dst_ref=w_got.at[exp], send_sem=w_s.at[d], recv_sem=w_r.at[d],
            device_id=(sky, peers[d]), device_id_type=MESH,
        )

    for d in range(1, N_EXP):
        meta(d).start()
    m_got[exp] = m_buf[...]

    for d in range(1, N_EXP):
        send_w(d).start()

    def start_halo(e, _):
        halo(0, e).start()
        halo(1, e).start()
        return 0

    lax.fori_loop(0, EXPS, start_halo, 0)
    own_w = pltpu.make_async_copy(w_buf.at[exp], w_got.at[exp], own_s.at[0])
    own_w.start()

    k3 = iota((ROWS, STEP), 1)
    k = lax.rem(k3, 80)
    source = jnp.where(
        k < 32, k, jnp.where(k < 48, k - 48, jnp.where(k < 68, k - 16, jnp.where(k < 72, k - 88, 1000)))
    )
    source = jnp.where(k3 < 240, source, 1000)
    source = jnp.where((source < 0) & (sky == 0), 1000, source)
    source = jnp.where((source >= ROWS) & (sky == N_SKY - 1), 1000, source)
    row_lag = source - iota((ROWS, STEP), 0) + RIM

    def row_band(b, _):
        def tap(t, band):
            return jnp.where(row_lag == t, row_taps[b, t], band)

        v_base[b] = lax.fori_loop(0, TAPS, tap, jnp.zeros((ROWS, STEP), F32))
        return 0

    lax.fori_loop(0, NB, row_band, 0)

    h_all[...] = jnp.zeros(h_all.shape, BF16)
    col_diff = iota((LANES, LANES), 0) - iota((LANES, LANES), 1) + RIM

    def col_band(b, _):
        for shift in (-1, 0, 1):
            lag = col_diff + LANES * shift

            def tap(t, band):
                return jnp.where(lag == t, col_taps[b, t], band)

            high, low = split(lax.fori_loop(0, TAPS, tap, jnp.zeros((LANES, LANES), F32)))
            for u in range(2):
                for third, band in enumerate((high, high, low)):
                    row = third * 2 * STEP + (u + 1 + shift) * LANES
                    h_all[b, row:row + LANES, u * LANES:(u + 1) * LANES] = band
        return 0

    lax.fori_loop(0, NB, col_band, 0)

    for part_z in (z_hi, z_lo):
        part_z[:, :, 0:LANES] = jnp.zeros((NB, ROWS, LANES), BF16)
        part_z[:, :, LANES + COLS:] = jnp.zeros((NB, ROWS, LANES), BF16)

    lane = iota((8, 2 * LANES), 1)
    lane_slot, lane_row = lane >> 3, lane & 7
    patch_row = iota((PR, 2 * LANES), 0)

    def select_rows(p, _):
        target = jnp.zeros((8, 2 * LANES), I32)
        for g in range(N_EXP):
            for j in range(SLOTS):
                target = jnp.where(lane_slot == g * SLOTS + j, m_smem[g, 1, p * SLOTS + j], target)
        target = (target + lane_row)[0:1]
        slots[p] = jnp.where(patch_row == target, 1.0, 0.0).astype(BF16)
        return 0


    def add_strips(got, acc, p):
        tiles = [
            got[g, m_smem[g, 0, p * SLOTS + j] & (2 * BLOCKS - 1)] for g in range(N_EXP) for j in range(SLOTS)
        ]
        high, low = split(jnp.concatenate(tiles, 0))
        both = jnp.dot(slots[p], jnp.concatenate([high, low], 1), preferred_element_type=F32)
        acc[p // NX, lax.rem(p, NX)] = both[:, 0:LANES] + both[:, LANES:]

    def halves(size):
        def half(ref, which):
            return ref.at[which * size:(which + 1) * size]

        return half

    def sums(acc, rows, x_first, land, land2, mid, send, recv, send2, recv2):
        if x_first:
            ring = Ring(NX, x, at_x, lambda o: acc.at[:, o, rows], halves(NZ // 2), land, send, recv)
            return ring, Direct(NZ, z, at_z, lambda o: mid.at[o], land2, send2, recv2)
        ring = Ring(NZ, z, at_z, lambda o: acc.at[o, :, rows], halves(NX // 2), land, send, recv)
        return ring, Direct(NX, x, at_x, lambda o: mid.at[o], land2, send2, recv2)

    u_a, u_az = sums(acc_w, pl.ds(0, 64), True, land_ua, land_uaz, mid_ua, ua_s, ua_r, uaz_s, uaz_r)
    u_b, u_bx = sums(acc_w, pl.ds(64, 64), False, land_ub, land_ubx, mid_ub, ub_s, ub_r, ubx_s, ubx_r)
    a_x, a_z, b_z, b_x = [], [], [], []
    for i in range(A_PARTS):
        rows = pl.ds(i * A_ROWS, A_ROWS)
        a_x.append(Ring(
            NX, x, at_x, lambda o, rows=rows: acc_v.at[:, o, rows], halves(NZ // 2),
            land_a.at[i], ax_s.at[i], ax_r.at[i],
        ))
        a_z.append(Ring(
            NZ, z, at_z, lambda o, i=i: mid_a.at[i, o], halves(A_ROWS // 2),
            land_az.at[i], az_s.at[i], az_r.at[i],
        ))
    for i in range(B_PARTS):
        rows = pl.ds(A_PARTS * A_ROWS + i * B_ROWS, B_ROWS)
        b_z.append(Ring(
            NZ, z, at_z, lambda o, rows=rows: acc_v.at[o, :, rows], halves(NX // 2),
            land_b.at[i], bz_s.at[i], bz_r.at[i],
        ))
        b_x.append(Direct(NX, x, at_x, lambda o, i=i: mid_b.at[i, o], land_bx.at[i], bx_s.at[i], bx_r.at[i]))

    def send_v(c, d):
        span = pl.ds(c * (8 * SEND), 8 * SEND)
        return pltpu.make_async_remote_copy(
            src_ref=v_buf.at[peers[d], span], dst_ref=v_got.at[exp, span],
            send_sem=v_s.at[c, d], recv_sem=v_r.at[c, d],
            device_id=(sky, peers[d]), device_id_type=MESH,
        )

    third = iota((NB * ROWS, STEP), 1) >= 160
    low_rows = iota((8, STEP), 0) < 4

    def exposure(e, _):
        @pl.when(e == SLOTS_AT)
        def _():
            for d in range(1, N_EXP):
                meta(d).wait_recv()
            table = pltpu.make_async_copy(m_got, m_smem, own_s.at[1])
            table.start()
            table.wait()
            lax.fori_loop(0, N_SKY, select_rows, 0)

        @pl.when(e == WEIGHTS_AT)
        def _():
            for d in range(1, N_EXP):
                send_w(d).wait_recv()
            own_w.wait()

            def send_held(c, _):
                for d in range(1, N_EXP):
                    send_v(c, d).start()
                return 0

            lax.fori_loop(0, WEIGHTS_AT // SEND, send_held, 0)

            def add_weights(p, _):
                add_strips(w_got, acc_w, p)
                return 0

            lax.fori_loop(0, N_SKY, add_weights, 0, unroll=4)
            u_b.begin()
            u_a.begin()

        halo(0, e).wait_recv()
        halo(1, e).wait_recv()
        table_row = coef_index[e]
        bands = [coef_table[b, table_row] * v_base[b] for b in range(NB)]
        high, low = split(jnp.concatenate(bands, 0))
        left = jnp.where(third, low.astype(F32), high.astype(F32)).astype(BF16)
        for j in range(NSTEP):
            part, at = divmod(j * STEP, HALF)
            cols = slice(at, at + STEP)
            up = h_recv[0, e, 2 * part:2 * part + 2, :, cols].reshape(16, STEP)
            down = h_recv[1, e, 2 * part:2 * part + 2, :, cols].reshape(16, STEP)
            up4, down4 = h_recv[0, e, 4, :, cols], h_recv[1, e, 4, :, cols]
            if part == 0:
                rest = jnp.where(low_rows, down4, up4)
            else:
                rest = pltpu.roll(jnp.where(low_rows, up4, down4), 4, 0)
            rows = jnp.concatenate(
                [image[e, :, j * STEP:(j + 1) * STEP], up, down, rest, jnp.zeros((8, STEP), F32)], 0
            )
            x_hi, x_lo = split(rows)
            right = jnp.concatenate([x_hi, x_lo, x_hi, jnp.zeros((16, STEP), BF16)], 0)
            high_z, low_z = split(jnp.dot(left, right, preferred_element_type=F32))
            at = LANES + j * STEP
            z_hi[:, :, at:at + STEP] = high_z.reshape(NB, ROWS, STEP)
            z_lo[:, :, at:at + STEP] = low_z.reshape(NB, ROWS, STEP)

        total = jnp.zeros((NSTEP * ROWS, STEP), F32)
        for b in range(NB):
            highs = jnp.concatenate([z_hi[b, :, j * STEP:(j + 2) * STEP] for j in range(NSTEP)], 0)
            lows = jnp.concatenate([z_lo[b, :, j * STEP:(j + 2) * STEP] for j in range(NSTEP)], 0)
            total += jnp.dot(jnp.concatenate([highs, lows, highs], 1), h_all[b], preferred_element_type=F32)
        for j in range(NSTEP):
            part = j // 4
            for u in range(2):
                q = (j % 4) * 2 + u
                for r in range(4):
                    row = j * ROWS + r * 8
                    strip = (e * 4 + r) * 2 + part
                    v_buf[q, strip] = total[row:row + 8, u * LANES:(u + 1) * LANES] * w_buf[q, strip]

        @pl.when((lax.rem(e, SEND) == SEND - 1) & (e >= WEIGHTS_AT))
        def _():
            for d in range(1, N_EXP):
                send_v(e // SEND, d).start()

        return 0

    lax.fori_loop(0, EXPS, exposure, 0)
    own_v = pltpu.make_async_copy(v_buf.at[exp], v_got.at[exp], own_s.at[2])
    own_v.start()

    u_b.advance(1)
    u_a.advance(1)
    u_b.advance(2)
    mid_ua[...] = u_a.total()
    u_az.begin()
    u_b.advance(3)
    mid_ub[...] = u_b.total()
    u_bx.begin()

    def arrived_v(c, _):
        for d in range(1, N_EXP):
            send_v(c, d).wait_recv()
        return 0

    lax.fori_loop(0, CHUNKS, arrived_v, 0)
    own_v.wait()

    def add_values(distance):
        owner = lax.rem(z + distance, NZ)

        def add(px, _):
            add_strips(v_got, acc_v, owner * NX + px)
            return 0

        lax.fori_loop(0, NX, add, 0, unroll=True)

    add_values(4)
    for ring in b_z:
        ring.begin(0)
    add_values(3)
    add_values(5)
    for ring in b_z:
        ring.begin(1)
    for distance in (2, 6, 1, 7, 0):
        add_values(distance)
    for ring in a_x:
        ring.begin()
    fin_w[0:64] = u_az.total()
    fin_w[64:128] = u_bx.total()

    def rows_copy(fin, land, send, recv, d):
        return pltpu.make_async_remote_copy(
            src_ref=fin.at[pl.ds(pl.multiple_of(peers[d] * 16, 16), 16)],
            dst_ref=land.at[exp],
            send_sem=send.at[d], recv_sem=recv.at[d],
            device_id=(sky, peers[d]), device_id_type=MESH,
        )

    mine = pl.ds(pl.multiple_of(exp * 16, 16), 16)
    for d in range(1, N_EXP):
        rows_copy(fin_w, rows_w, rw_s, rw_r, d).start()
    rows_w[exp] = fin_w[mine]
    for ring in b_z:
        ring.advance(1)
    for ring in a_x:
        ring.advance(1)
    for ring in b_z:
        ring.advance(2)
    for i in range(A_PARTS):
        mid_a[i] = a_x[i].total()
        a_z[i].begin()
    for ring in b_z:
        ring.advance(3)
    for ring in a_z:
        ring.advance(1)
    for i in range(B_PARTS):
        mid_b[i] = b_z[i].total()
        b_x[i].begin()
    for step in (2, 3):
        for ring in a_z:
            ring.advance(step)
    for i in range(B_PARTS):
        row = A_PARTS * A_ROWS + i * B_ROWS
        fin_v[row:row + B_ROWS] = b_x[i].total()
    for i in range(A_PARTS):
        fin_v[i * A_ROWS:(i + 1) * A_ROWS] = a_z[i].total()
    for d in range(1, N_EXP):
        rows_copy(fin_v, rows_v, rv_s, rv_r, d).start()
    rows_v[exp] = fin_v[mine]
    for d in range(1, N_EXP):
        rows_copy(fin_w, rows_w, rw_s, rw_r, d).wait()
    for q in range(N_EXP):
        out[1, :, q * LANES:(q + 1) * LANES] = rows_w[q]

    def end_halo(e, _):
        halo(0, e).wait_send()
        halo(1, e).wait_send()
        return 0

    lax.fori_loop(0, EXPS, end_halo, 0)
    for d in range(1, N_EXP):
        meta(d).wait_send()
        send_w(d).wait_send()

    def end_v(c, _):
        for d in range(1, N_EXP):
            send_v(c, d).wait_send()
        return 0

    lax.fori_loop(0, CHUNKS, end_v, 0)
    for ring in (u_a, u_az, u_b, u_bx, *a_x, *a_z, *b_z, *b_x):
        ring.drain()
    for d in range(1, N_EXP):
        rows_copy(fin_v, rows_v, rv_s, rv_r, d).wait()
    for q in range(N_EXP):
        out[0, :, q * LANES:(q + 1) * LANES] = rows_v[q]


def per_device(image, variance, coef_index, coef_table, row_taps, col_taps, destination, offset):
    vmem, smem, anywhere = (pl.BlockSpec(memory_space=s) for s in (pltpu.VMEM, pltpu.SMEM, pl.ANY))
    dma = pltpu.SemaphoreType.DMA

    def held(*shape, dtype=F32):
        return pltpu.VMEM(shape, dtype)

    strips = (N_EXP, 2 * BLOCKS, 8, LANES)
    sums = pl.pallas_call(
        coadd_kernel,
        out_shape=jax.ShapeDtypeStruct((2, PR // N_EXP, HALF), F32),
        in_specs=[anywhere] * 2 + [vmem] * 2 + [smem] * 4,
        out_specs=vmem,
        scratch_shapes=[
            held(EXPS, ROWS, COLS), held(EXPS, ROWS, COLS),
            held(2, EXPS, 5, 8, HALF), held(2, EXPS, 5, 8, HALF),
            held(*strips), held(*strips), held(*strips), held(*strips),
            held(8, LANES, dtype=I32), held(N_EXP, 8, LANES, dtype=I32),
            pltpu.SMEM((N_EXP, 8, LANES), I32),
            held(N_SKY, PR, 2 * LANES, dtype=BF16),
            held(NB, ROWS, COLS + 2 * LANES, dtype=BF16),
            held(NB, ROWS, COLS + 2 * LANES, dtype=BF16),
            held(NB, 6 * STEP, STEP, dtype=BF16),
            held(NB, ROWS, STEP),
            held(NZ, NX, PR, LANES), held(NZ, NX, PR, LANES),
            held(2, 2, NZ, 64, LANES), held(NZ, 64, LANES),
            held(2, 4, NX, 64, LANES), held(NX, 64, LANES),
            held(A_PARTS, 2, 2, NZ, A_ROWS, LANES), held(A_PARTS, 2, 4, A_ROWS, LANES),
            held(B_PARTS, 2, 4, NX, B_ROWS, LANES), held(B_PARTS, NX, B_ROWS, LANES),
            held(NZ, 64, LANES), held(NX, 64, LANES), held(A_PARTS, NZ, A_ROWS, LANES), held(B_PARTS, NX, B_ROWS, LANES),
            held(PR, LANES), held(PR, LANES),
            held(N_EXP, PR // N_EXP, LANES), held(N_EXP, PR // N_EXP, LANES),
            dma((2,)), dma((2, EXPS)), dma((2, EXPS)),
            dma((N_EXP,)), dma((N_EXP,)),
            dma((CHUNKS, N_EXP)), dma((CHUNKS, N_EXP)),
            dma((N_EXP,)), dma((N_EXP,)),
            dma((3,)),
        ] + [
            dma(shape)
            for shape in ((2, 3), (NZ,), (2, 5), (NX,), (A_PARTS, 2, 3), (A_PARTS, 2, 5), (B_PARTS, 2, 5), (B_PARTS, NX), (N_EXP,), (N_EXP,))
            for _ in range(2)
        ],
        compiler_params=pltpu.CompilerParams(
            collective_id=0, has_side_effects=True, vmem_limit_bytes=60 * 1024 * 1024
        ),
    )(
        image, variance, destination.reshape(1, -1), offset.reshape(1, -1),
        coef_index, coef_table.T, row_taps, col_taps,
    )
    return sums[0] / (1.0 + sums[1]), sums[1]


def solution(mesh):
    placed = (
        P("exp", "sky", None),
        P("exp", "sky", None),
        P("exp"),
        P(),
        P(),
        P(),
        P("exp", "sky", None, None),
        P("exp", "sky", None),
    )
    return jax.shard_map(
        per_device,
        mesh=mesh,
        in_specs=placed,
        out_specs=(P(("sky", "exp"), None), P(("sky", "exp"), None)),
        check_vma=False,
    )
```

```python
import jax
import jax.numpy as jnp
from jax import lax
from jax.experimental import pallas as pl
from jax.experimental.pallas import tpu as pltpu
from jax.sharding import PartitionSpec as P

MESH = pl.DeviceIdType.MESH
F32, BF16, I32 = jnp.float32, jnp.bfloat16, jnp.int32

NB, TAPS, RIM = 5, 41, 20
N_SKY, N_EXP, NX, NZ = 32, 8, 4, 8
EXPS, ROWS, COLS, HALF = 8, 32, 2048, 1024
BLOCKS = EXPS * ROWS // 8
LANES = 128
PR, PATCH_ROWS = 128, 4096
SEND = 4
CHUNKS = EXPS // SEND
SLOTS_AT = 3
RELEASE_AT = 5
WEIGHTS_AT = 6
A_PARTS, A_ROWS = 1, 64
B_PARTS, B_ROWS = 1, 64
STEP = 256
NSTEP = COLS // STEP


def iota(shape, dim):
    return lax.broadcasted_iota(I32, shape, dim)


def greet(devices):
    barrier = pltpu.get_barrier_semaphore()
    for device in devices:
        pl.semaphore_signal(barrier, inc=1, device_id=device, device_id_type=MESH)
    pl.semaphore_wait(barrier, len(devices))


def split(value):
    high = value.astype(BF16)
    return high, (value - high.astype(F32)).astype(BF16)

SLOTS = 4
EMPTY = -4096


def strip_table(dest, offs):
    sub, lane = iota((64, LANES), 0), iota((64, LANES), 1)
    line = jnp.concatenate([dest, jnp.full((1, 64), -1, I32)], 1)
    shift = jnp.concatenate([offs, jnp.zeros((1, 64), I32)], 1)
    diagonal = sub == lane
    patch = jnp.sum(jnp.where(diagonal, line, 0), 1, keepdims=True)
    first = jnp.sum(jnp.where(diagonal, shift, 0), 1, keepdims=True)
    rank = jnp.sum(jnp.where((patch == line) & (lane < sub), 1, 0), 1, keepdims=True)
    here = patch * SLOTS + rank == lane
    strip = jnp.sum(jnp.where(here, sub, 0), 0, keepdims=True)
    start = jnp.sum(jnp.where(here, first - EMPTY, 0), 0, keepdims=True) + EMPTY
    row = iota((8, LANES), 0)
    return jnp.where(row == 0, strip, jnp.where(row == 1, start, 0))


class Ring:
    def __init__(self, size, me, target, chunk, half, land, send, recv):
        self.size, self.me, self.target = size, me, target
        self.chunk, self.half, self.land = chunk, half, land
        self.send, self.recv = send, recv
        self.steps = size // 2

    def owner(self, way, distance):
        return lax.rem(self.me + (distance if way == 0 else self.size - distance), self.size)

    def copy(self, src, dst, way, number):
        return pltpu.make_async_remote_copy(
            src_ref=src, dst_ref=dst, send_sem=self.send.at[way, number], recv_sem=self.recv.at[way, number],
            device_id=self.target(self.owner(way, 1)), device_id_type=MESH,
        )

    def copies(self, way, step):
        own = self.chunk(self.owner(way, self.steps - step))
        here = self.land.at[way, step]
        if step == 0:
            return [self.copy(self.half(own, way), self.half(here, way), way, 0)], []
        came = self.land.at[way, step - 1]
        if step == 1:
            early = [self.copy(self.half(own, 1 - way), self.half(here, 1 - way), way, 1)]
            return early, [self.copy(self.half(came, way), self.half(here, way), way, 2)]
        return [], [self.copy(came, here, way, step + 1)]

    def begin(self, *steps):
        for step in steps or (0, 1):
            for way in (0, 1):
                for copy in self.copies(way, step)[0]:
                    copy.start()

    def arrived(self, way, step):
        early, late = self.copies(way, step)
        for copy in early + late:
            copy.wait_recv()

    def advance(self, step):
        for way in (0, 1):
            self.arrived(way, step - 1)
            came = self.land.at[way, step - 1]
            own = self.chunk(self.owner(way, self.steps - step))
            if step == 1:
                came, own = self.half(came, way), self.half(own, way)
            came[...] = came[...] + own[...]
            for copy in self.copies(way, step)[1]:
                copy.start()

    def total(self):
        last = self.steps - 1
        for way in (0, 1):
            self.arrived(way, last)
        return self.chunk(self.me)[...] + self.land[0, last] + self.land[1, last]

    def drain(self):
        for step in range(self.steps):
            for way in (0, 1):
                early, late = self.copies(way, step)
                for copy in early + late:
                    copy.wait_send()


class Direct:
    def __init__(self, size, me, target, chunk, land, send, recv):
        self.size, self.me, self.target = size, me, target
        self.chunk, self.land, self.send, self.recv = chunk, land, send, recv

    def copy(self, d):
        owner = lax.rem(self.me + d, self.size)
        return pltpu.make_async_remote_copy(
            src_ref=self.chunk(owner), dst_ref=self.land.at[d], send_sem=self.send.at[d], recv_sem=self.recv.at[d],
            device_id=self.target(owner), device_id_type=MESH,
        )

    def begin(self):
        for d in range(1, self.size):
            self.copy(d).start()

    def total(self):
        total = self.chunk(self.me)[...]
        for d in range(1, self.size):
            self.copy(d).wait_recv()
            total = total + self.land[d]
        return total

    def drain(self):
        for d in range(1, self.size):
            self.copy(d).wait_send()


def coadd_kernel(
    image_in, variance_in, dest, offs, coef_index, coef_table, row_taps, col_taps,
    out,
    image, variance, h_send, h_recv, w_buf, v_buf, w_got, v_got, m_buf, m_got, m_smem, slots,
    z_hi, z_lo, h_all, v_base, acc_w, acc_v,
    land_ua, land_uaz, land_ub, land_ubx, land_a, land_az, land_b, land_bx, mid_ua, mid_ub, mid_a, mid_b, fin_w, fin_v, rows_w, rows_v,
    load_s, halo_s, halo_r, w_s, w_r, v_s, v_r, m_s, m_r, own_s,
    ua_s, ua_r, uaz_s, uaz_r, ub_s, ub_r, ubx_s, ubx_r, ax_s, ax_r, az_s, az_r, bz_s, bz_r, bx_s, bx_r, rw_s, rw_r, rv_s, rv_r,
):
    sky, exp = lax.axis_index("sky"), lax.axis_index("exp")
    z, x = sky // NX, lax.rem(sky, NX)
    after, before = lax.rem(sky + 1, N_SKY), lax.rem(sky + N_SKY - 1, N_SKY)
    peers = [lax.rem(exp + d, N_EXP) for d in range(N_EXP)]

    def at_x(other):
        return (z * NX + other, exp)

    def at_z(other):
        return (other * NX + x, exp)

    load_image = pltpu.make_async_copy(image_in, image, load_s.at[0])
    load_variance = pltpu.make_async_copy(variance_in, variance, load_s.at[1])
    load_variance.start()
    load_image.start()

    partners = [(after, exp), (before, exp)] + [(sky, q) for q in peers[1:]] + [
        at_x(lax.rem(x + d, NX)) for d in range(1, NX)
    ] + [at_z(lax.rem(z + d, NZ)) for d in range(1, NZ)]
    barrier = pltpu.get_barrier_semaphore()
    for device in partners:
        pl.semaphore_signal(barrier, inc=1, device_id=device, device_id_type=MESH)

    load_variance.wait()

    def weights(eb, _):
        e, rb = eb // 4, lax.rem(eb, 4)
        rows = pl.ds(pl.multiple_of(rb * 8, 8), 8)
        for part in range(2):
            for q in range(N_EXP):
                lane = part * HALF + q * LANES
                w_buf[q, eb * 2 + part] = 1.0 / variance[e, rows, lane:lane + LANES]
        return 0

    lax.fori_loop(0, BLOCKS, weights, 0)
    load_image.wait()
    low_half = iota((8, HALF), 0) < 4

    def pack(e, _):
        h_send[0, e, 0] = image[e, 16:24, 0:HALF]
        h_send[0, e, 1] = image[e, 24:32, 0:HALF]
        h_send[0, e, 2] = image[e, 16:24, HALF:COLS]
        h_send[0, e, 3] = image[e, 24:32, HALF:COLS]
        h_send[0, e, 4] = jnp.where(
            low_half, pltpu.roll(image[e, 8:16, HALF:COLS], 4, 0), image[e, 8:16, 0:HALF]
        )
        h_send[1, e, 0] = image[e, 0:8, 0:HALF]
        h_send[1, e, 1] = image[e, 8:16, 0:HALF]
        h_send[1, e, 2] = image[e, 0:8, HALF:COLS]
        h_send[1, e, 3] = image[e, 8:16, HALF:COLS]
        h_send[1, e, 4] = jnp.where(
            low_half, image[e, 16:24, 0:HALF], pltpu.roll(image[e, 16:24, HALF:COLS], 4, 0)
        )
        return 0

    lax.fori_loop(0, EXPS, pack, 0)
    m_buf[...] = strip_table(dest[...], offs[...])
    pl.semaphore_wait(barrier, len(partners))

    def halo(direction, e):
        return pltpu.make_async_remote_copy(
            src_ref=h_send.at[direction, e],
            dst_ref=h_recv.at[direction, e],
            send_sem=halo_s.at[direction, e],
            recv_sem=halo_r.at[direction, e],
            device_id=(after if direction == 0 else before, exp),
            device_id_type=MESH,
        )

    def meta(d):
        return pltpu.make_async_remote_copy(
            src_ref=m_buf, dst_ref=m_got.at[exp], send_sem=m_s.at[d], recv_sem=m_r.at[d],
            device_id=(sky, peers[d]), device_id_type=MESH,
        )

    def send_w(d):
        return pltpu.make_async_remote_copy(
            src_ref=w_buf.at[peers[d]], dst_ref=w_got.at[exp], send_sem=w_s.at[d], recv_sem=w_r.at[d],
            device_id=(sky, peers[d]), device_id_type=MESH,
        )

    for d in range(1, N_EXP):
        meta(d).start()
    m_got[exp] = m_buf[...]

    for d in range(1, N_EXP):
        send_w(d).start()

    def start_halo(e, _):
        halo(0, e).start()
        halo(1, e).start()
        return 0

    lax.fori_loop(0, EXPS, start_halo, 0)
    own_w = pltpu.make_async_copy(w_buf.at[exp], w_got.at[exp], own_s.at[0])
    own_w.start()

    k3 = iota((ROWS, STEP), 1)
    k = lax.rem(k3, 80)
    source = jnp.where(
        k < 32, k, jnp.where(k < 48, k - 48, jnp.where(k < 68, k - 16, jnp.where(k < 72, k - 88, 1000)))
    )
    source = jnp.where(k3 < 240, source, 1000)
    source = jnp.where((source < 0) & (sky == 0), 1000, source)
    source = jnp.where((source >= ROWS) & (sky == N_SKY - 1), 1000, source)
    row_lag = source - iota((ROWS, STEP), 0) + RIM

    def row_band(b, _):
        def tap(t, band):
            return jnp.where(row_lag == t, row_taps[b, t], band)

        v_base[b] = lax.fori_loop(0, TAPS, tap, jnp.zeros((ROWS, STEP), F32))
        return 0

    lax.fori_loop(0, NB, row_band, 0)

    h_all[...] = jnp.zeros(h_all.shape, BF16)
    col_diff = iota((LANES, LANES), 0) - iota((LANES, LANES), 1) + RIM

    def col_band(b, _):
        for shift in (-1, 0, 1):
            lag = col_diff + LANES * shift

            def tap(t, band):
                return jnp.where(lag == t, col_taps[b, t], band)

            high, low = split(lax.fori_loop(0, TAPS, tap, jnp.zeros((LANES, LANES), F32)))
            for u in range(2):
                for third, band in enumerate((high, high, low)):
                    row = third * 2 * STEP + (u + 1 + shift) * LANES
                    h_all[b, row:row + LANES, u * LANES:(u + 1) * LANES] = band
        return 0

    lax.fori_loop(0, NB, col_band, 0)

    for part_z in (z_hi, z_lo):
        part_z[:, :, 0:LANES] = jnp.zeros((NB, ROWS, LANES), BF16)
        part_z[:, :, LANES + COLS:] = jnp.zeros((NB, ROWS, LANES), BF16)

    lane = iota((8, 2 * LANES), 1)
    lane_slot, lane_row = lane >> 3, lane & 7
    patch_row = iota((PR, 2 * LANES), 0)

    def select_rows(p, _):
        target = jnp.zeros((8, 2 * LANES), I32)
        for g in range(N_EXP):
            for j in range(SLOTS):
                target = jnp.where(lane_slot == g * SLOTS + j, m_smem[g, 1, p * SLOTS + j], target)
        target = (target + lane_row)[0:1]
        slots[p] = jnp.where(patch_row == target, 1.0, 0.0).astype(BF16)
        return 0


    def add_strips(got, acc, p):
        tiles = [
            got[g, m_smem[g, 0, p * SLOTS + j] & (2 * BLOCKS - 1)] for g in range(N_EXP) for j in range(SLOTS)
        ]
        high, low = split(jnp.concatenate(tiles, 0))
        both = jnp.dot(slots[p], jnp.concatenate([high, low], 1), preferred_element_type=F32)
        acc[p // NX, lax.rem(p, NX)] = both[:, 0:LANES] + both[:, LANES:]

    def halves(size):
        def half(ref, which):
            return ref.at[which * size:(which + 1) * size]

        return half

    def sums(acc, rows, x_first, land, land2, mid, send, recv, send2, recv2):
        if x_first:
            ring = Ring(NX, x, at_x, lambda o: acc.at[:, o, rows], halves(NZ // 2), land, send, recv)
            return ring, Direct(NZ, z, at_z, lambda o: mid.at[o], land2, send2, recv2)
        ring = Ring(NZ, z, at_z, lambda o: acc.at[o, :, rows], halves(NX // 2), land, send, recv)
        return ring, Direct(NX, x, at_x, lambda o: mid.at[o], land2, send2, recv2)

    u_a, u_az = sums(acc_w, pl.ds(0, 64), True, land_ua, land_uaz, mid_ua, ua_s, ua_r, uaz_s, uaz_r)
    u_b, u_bx = sums(acc_w, pl.ds(64, 64), False, land_ub, land_ubx, mid_ub, ub_s, ub_r, ubx_s, ubx_r)
    a_x, a_z, b_z, b_x = [], [], [], []
    for i in range(A_PARTS):
        rows = pl.ds(i * A_ROWS, A_ROWS)
        a_x.append(Ring(
            NX, x, at_x, lambda o, rows=rows: acc_v.at[:, o, rows], halves(NZ // 2),
            land_a.at[i], ax_s.at[i], ax_r.at[i],
        ))
        a_z.append(Ring(
            NZ, z, at_z, lambda o, i=i: mid_a.at[i, o], halves(A_ROWS // 2),
            land_az.at[i], az_s.at[i], az_r.at[i],
        ))
    for i in range(B_PARTS):
        rows = pl.ds(A_PARTS * A_ROWS + i * B_ROWS, B_ROWS)
        b_z.append(Ring(
            NZ, z, at_z, lambda o, rows=rows: acc_v.at[o, :, rows], halves(NX // 2),
            land_b.at[i], bz_s.at[i], bz_r.at[i],
        ))
        b_x.append(Direct(NX, x, at_x, lambda o, i=i: mid_b.at[i, o], land_bx.at[i], bx_s.at[i], bx_r.at[i]))

    def send_v(c, d):
        span = pl.ds(c * (8 * SEND), 8 * SEND)
        return pltpu.make_async_remote_copy(
            src_ref=v_buf.at[peers[d], span], dst_ref=v_got.at[exp, span],
            send_sem=v_s.at[c, d], recv_sem=v_r.at[c, d],
            device_id=(sky, peers[d]), device_id_type=MESH,
        )

    third = iota((NB * ROWS, STEP), 1) >= 160
    low_rows = iota((8, STEP), 0) < 4

    def exposure(e, _):
        @pl.when(e == SLOTS_AT)
        def _():
            for d in range(1, N_EXP):
                meta(d).wait_recv()
            table = pltpu.make_async_copy(m_got, m_smem, own_s.at[1])
            table.start()
            table.wait()
            lax.fori_loop(0, N_SKY, select_rows, 0)

        @pl.when(e == WEIGHTS_AT)
        def _():
            for d in range(1, N_EXP):
                send_w(d).wait_recv()
            own_w.wait()


            def add_weights(p, _):
                add_strips(w_got, acc_w, p)
                return 0

            lax.fori_loop(0, N_SKY, add_weights, 0, unroll=4)
            u_b.begin()
            u_a.begin()

        halo(0, e).wait_recv()
        halo(1, e).wait_recv()
        table_row = coef_index[e]
        bands = [coef_table[b, table_row] * v_base[b] for b in range(NB)]
        high, low = split(jnp.concatenate(bands, 0))
        left = jnp.where(third, low.astype(F32), high.astype(F32)).astype(BF16)
        for j in range(NSTEP):
            part, at = divmod(j * STEP, HALF)
            cols = slice(at, at + STEP)
            up = h_recv[0, e, 2 * part:2 * part + 2, :, cols].reshape(16, STEP)
            down = h_recv[1, e, 2 * part:2 * part + 2, :, cols].reshape(16, STEP)
            up4, down4 = h_recv[0, e, 4, :, cols], h_recv[1, e, 4, :, cols]
            if part == 0:
                rest = jnp.where(low_rows, down4, up4)
            else:
                rest = pltpu.roll(jnp.where(low_rows, up4, down4), 4, 0)
            rows = jnp.concatenate(
                [image[e, :, j * STEP:(j + 1) * STEP], up, down, rest, jnp.zeros((8, STEP), F32)], 0
            )
            x_hi, x_lo = split(rows)
            right = jnp.concatenate([x_hi, x_lo, x_hi, jnp.zeros((16, STEP), BF16)], 0)
            high_z, low_z = split(jnp.dot(left, right, preferred_element_type=F32))
            at = LANES + j * STEP
            z_hi[:, :, at:at + STEP] = high_z.reshape(NB, ROWS, STEP)
            z_lo[:, :, at:at + STEP] = low_z.reshape(NB, ROWS, STEP)

        total = jnp.zeros((NSTEP * ROWS, STEP), F32)
        for b in range(NB):
            highs = jnp.concatenate([z_hi[b, :, j * STEP:(j + 2) * STEP] for j in range(NSTEP)], 0)
            lows = jnp.concatenate([z_lo[b, :, j * STEP:(j + 2) * STEP] for j in range(NSTEP)], 0)
            total += jnp.dot(jnp.concatenate([highs, lows, highs], 1), h_all[b], preferred_element_type=F32)
        for j in range(NSTEP):
            part = j // 4
            for u in range(2):
                q = (j % 4) * 2 + u
                for r in range(4):
                    row = j * ROWS + r * 8
                    strip = (e * 4 + r) * 2 + part
                    v_buf[q, strip] = total[row:row + 8, u * LANES:(u + 1) * LANES] * w_buf[q, strip]

        @pl.when(e == RELEASE_AT)
        def _():
            for d in range(1, N_EXP):
                send_v(0, d).start()

        @pl.when(e == EXPS - 1)
        def _():
            for d in range(1, N_EXP):
                send_v(1, d).start()

        return 0

    lax.fori_loop(0, EXPS, exposure, 0)
    own_v = pltpu.make_async_copy(v_buf.at[exp], v_got.at[exp], own_s.at[2])
    own_v.start()

    u_b.advance(1)
    u_a.advance(1)
    u_b.advance(2)
    mid_ua[...] = u_a.total()
    u_az.begin()
    u_b.advance(3)
    mid_ub[...] = u_b.total()
    u_bx.begin()

    def arrived_v(c, _):
        for d in range(1, N_EXP):
            send_v(c, d).wait_recv()
        return 0

    lax.fori_loop(0, CHUNKS, arrived_v, 0)
    own_v.wait()

    def add_values(distance):
        owner = lax.rem(z + distance, NZ)

        def add(px, _):
            add_strips(v_got, acc_v, owner * NX + px)
            return 0

        lax.fori_loop(0, NX, add, 0, unroll=True)

    add_values(4)
    for ring in b_z:
        ring.begin(0)
    add_values(3)
    add_values(5)
    for ring in b_z:
        ring.begin(1)
    for distance in (2, 6, 1, 7, 0):
        add_values(distance)
    for ring in a_x:
        ring.begin()
    fin_w[0:64] = u_az.total()
    fin_w[64:128] = u_bx.total()

    def rows_copy(fin, land, send, recv, d):
        return pltpu.make_async_remote_copy(
            src_ref=fin.at[pl.ds(pl.multiple_of(peers[d] * 16, 16), 16)],
            dst_ref=land.at[exp],
            send_sem=send.at[d], recv_sem=recv.at[d],
            device_id=(sky, peers[d]), device_id_type=MESH,
        )

    mine = pl.ds(pl.multiple_of(exp * 16, 16), 16)
    for d in range(1, N_EXP):
        rows_copy(fin_w, rows_w, rw_s, rw_r, d).start()
    rows_w[exp] = fin_w[mine]
    for ring in b_z:
        ring.advance(1)
    for ring in a_x:
        ring.advance(1)
    for ring in b_z:
        ring.advance(2)
    for i in range(A_PARTS):
        mid_a[i] = a_x[i].total()
        a_z[i].begin()
    for ring in b_z:
        ring.advance(3)
    for ring in a_z:
        ring.advance(1)
    for i in range(B_PARTS):
        mid_b[i] = b_z[i].total()
        b_x[i].begin()
    for step in (2, 3):
        for ring in a_z:
            ring.advance(step)
    for i in range(B_PARTS):
        row = A_PARTS * A_ROWS + i * B_ROWS
        fin_v[row:row + B_ROWS] = b_x[i].total()
    for i in range(A_PARTS):
        fin_v[i * A_ROWS:(i + 1) * A_ROWS] = a_z[i].total()
    for d in range(1, N_EXP):
        rows_copy(fin_v, rows_v, rv_s, rv_r, d).start()
    rows_v[exp] = fin_v[mine]
    for d in range(1, N_EXP):
        rows_copy(fin_w, rows_w, rw_s, rw_r, d).wait()
    for q in range(N_EXP):
        out[1, :, q * LANES:(q + 1) * LANES] = rows_w[q]

    def end_halo(e, _):
        halo(0, e).wait_send()
        halo(1, e).wait_send()
        return 0

    lax.fori_loop(0, EXPS, end_halo, 0)
    for d in range(1, N_EXP):
        meta(d).wait_send()
        send_w(d).wait_send()

    def end_v(c, _):
        for d in range(1, N_EXP):
            send_v(c, d).wait_send()
        return 0

    lax.fori_loop(0, CHUNKS, end_v, 0)
    for ring in (u_a, u_az, u_b, u_bx, *a_x, *a_z, *b_z, *b_x):
        ring.drain()
    for d in range(1, N_EXP):
        rows_copy(fin_v, rows_v, rv_s, rv_r, d).wait()
    for q in range(N_EXP):
        out[0, :, q * LANES:(q + 1) * LANES] = rows_v[q]


def per_device(image, variance, coef_index, coef_table, row_taps, col_taps, destination, offset):
    vmem, smem, anywhere = (pl.BlockSpec(memory_space=s) for s in (pltpu.VMEM, pltpu.SMEM, pl.ANY))
    dma = pltpu.SemaphoreType.DMA

    def held(*shape, dtype=F32):
        return pltpu.VMEM(shape, dtype)

    strips = (N_EXP, 2 * BLOCKS, 8, LANES)
    sums = pl.pallas_call(
        coadd_kernel,
        out_shape=jax.ShapeDtypeStruct((2, PR // N_EXP, HALF), F32),
        in_specs=[anywhere] * 2 + [vmem] * 2 + [smem] * 4,
        out_specs=vmem,
        scratch_shapes=[
            held(EXPS, ROWS, COLS), held(EXPS, ROWS, COLS),
            held(2, EXPS, 5, 8, HALF), held(2, EXPS, 5, 8, HALF),
            held(*strips), held(*strips), held(*strips), held(*strips),
            held(8, LANES, dtype=I32), held(N_EXP, 8, LANES, dtype=I32),
            pltpu.SMEM((N_EXP, 8, LANES), I32),
            held(N_SKY, PR, 2 * LANES, dtype=BF16),
            held(NB, ROWS, COLS + 2 * LANES, dtype=BF16),
            held(NB, ROWS, COLS + 2 * LANES, dtype=BF16),
            held(NB, 6 * STEP, STEP, dtype=BF16),
            held(NB, ROWS, STEP),
            held(NZ, NX, PR, LANES), held(NZ, NX, PR, LANES),
            held(2, 2, NZ, 64, LANES), held(NZ, 64, LANES),
            held(2, 4, NX, 64, LANES), held(NX, 64, LANES),
            held(A_PARTS, 2, 2, NZ, A_ROWS, LANES), held(A_PARTS, 2, 4, A_ROWS, LANES),
            held(B_PARTS, 2, 4, NX, B_ROWS, LANES), held(B_PARTS, NX, B_ROWS, LANES),
            held(NZ, 64, LANES), held(NX, 64, LANES), held(A_PARTS, NZ, A_ROWS, LANES), held(B_PARTS, NX, B_ROWS, LANES),
            held(PR, LANES), held(PR, LANES),
            held(N_EXP, PR // N_EXP, LANES), held(N_EXP, PR // N_EXP, LANES),
            dma((2,)), dma((2, EXPS)), dma((2, EXPS)),
            dma((N_EXP,)), dma((N_EXP,)),
            dma((CHUNKS, N_EXP)), dma((CHUNKS, N_EXP)),
            dma((N_EXP,)), dma((N_EXP,)),
            dma((3,)),
        ] + [
            dma(shape)
            for shape in ((2, 3), (NZ,), (2, 5), (NX,), (A_PARTS, 2, 3), (A_PARTS, 2, 5), (B_PARTS, 2, 5), (B_PARTS, NX), (N_EXP,), (N_EXP,))
            for _ in range(2)
        ],
        compiler_params=pltpu.CompilerParams(
            collective_id=0, has_side_effects=True, vmem_limit_bytes=60 * 1024 * 1024
        ),
    )(
        image, variance, destination.reshape(1, -1), offset.reshape(1, -1),
        coef_index, coef_table.T, row_taps, col_taps,
    )
    return sums[0] / (1.0 + sums[1]), sums[1]


def solution(mesh):
    placed = (
        P("exp", "sky", None),
        P("exp", "sky", None),
        P("exp"),
        P(),
        P(),
        P(),
        P("exp", "sky", None, None),
        P("exp", "sky", None),
    )
    return jax.shard_map(
        per_device,
        mesh=mesh,
        in_specs=placed,
        out_specs=(P(("sky", "exp"), None), P(("sky", "exp"), None)),
        check_vma=False,
    )
```
